256 devices in a mesh: group: 8 (over z), rank: 32 (over y, x, core).
Axes of the slice: x: 4, y: 4, z: 8, core: 2. Of those that a mesh axis runs over, the one named last changes fastest.
Arguments:
- queries: bfloat16 [4096, 64, 576], P(('group', 'rank')), parts along dimension 0, may hold values from -20 to 20
- cache_pool: bfloat16 [4096, 32, 576], P(('group', 'rank')), parts along dimension 0, may hold values from -6 to 6
- lengths: int32 [4096], P(('group', 'rank')), parts along dimension 0, may hold values from 0 to 128, as said below
- block_table: int32 [4096, 4], P(('group', 'rank')), parts along dimension 0, may hold values from 0 to 15, as said below
- residual: bfloat16 [4096, 7168], P(('group', 'rank')), parts along dimension 0, may hold values from -3 to 3
- norm_gain: bfloat16 [7168], replicated, may hold values from 0.099609375 to 1.8984375
- uv_weight: bfloat16 [64, 512, 128], P('rank'), may hold values from -0.25 to 0.25
- out_weight: bfloat16 [8192, 7168], P(None, 'rank'), may hold values from -0.0625 to 0.0625
- gate_weight: bfloat16 [7168, 9216], P(None, 'rank'), may hold values from -0.0625 to 0.0625
- up_weight: bfloat16 [7168, 9216], P(None, 'rank'), may hold values from -0.0625 to 0.0625
Outputs:
- mixed: bfloat16 [4096, 7168], P(('group', 'rank')), parts along dimension 0
- activ: bfloat16 [4096, 9216], P('group', 'rank'), parts along dimension 0
The draws below stay inside these ranges and needn't reach their ends.
There are 8 independent parts, one for each index of `group`. The reference program is written for one: setup_inputs(seed, part) draws one part's arguments, and reference() takes and returns one part's arrays. A program takes and returns all parts, laid end to end along the dimension named above; an argument that names none is the same for every part. Nothing has to cross between parts.
Inputs may be any that keep to these rules, and one draw needn't show every extreme that they name: `lengths`: the live slots of each rank are its first ones, at least one a rank; some rank has all 16 slots live and some rank exactly one. A live slot holds 1 to 128 tokens and the longest reaches that in every draw. `block_table`: A slot's first ceil(lengths / 32) entries name distinct pages of its own rank, no page shared between slots; the other entries are 0.
All inputs are finite; a program needn't handle non-finite values.
Results may differ from the reference program's by a relative error of at most 0.0075.
Values may be sent and summed in bfloat16 or wider, within the bound.
A program may use at most 64 MiB of HBM per device.

```python
import jax
import jax.numpy as jnp
from jax import lax

D = 7168
H = 64
LAT = 512
ROPE = 64
HD = 128
FF = 9216
R_DEV = 16
PAGE = 32
MAXP = 4
PAGES_DEV = 16
ROWS = 512
POOL = 512
N_RANK = 32


def slot_layout(key):
    key = jax.random.fold_in(key, 11)
    streams = jax.random.split(key, 5)
    order = jax.random.permutation(streams[0], N_RANK)
    live = jax.random.randint(streams[1], (N_RANK,), 1, R_DEV + 1)
    live = live.at[order[0]].set(R_DEV)
    live = live.at[order[1]].set(1)
    slots = jnp.arange(R_DEV, dtype=jnp.int32)
    ranking = jax.vmap(lambda k: jax.random.permutation(k, R_DEV))(jax.random.split(streams[2], N_RANK))
    active = slots[None, :] < live[:, None]
    ahead = jnp.sum((ranking[:, None, :] < ranking[:, :, None]) & active[:, None, :], axis=2).astype(jnp.int32)
    spare = PAGES_DEV - live
    counts = 1 + jnp.clip(spare[:, None] - (MAXP - 1) * ahead, 0, MAXP - 1)
    counts = jnp.where(active, counts, 0)
    ending = jax.random.randint(streams[3], (N_RANK, R_DEV), 1, PAGE + 1)
    ending = jnp.where(counts == MAXP, PAGE, ending)
    sizes_all = jnp.where(active, (counts - 1) * PAGE + ending, 0)
    starts = jnp.cumsum(counts, axis=1) - counts
    shuffle = jax.vmap(lambda k: jax.random.permutation(k, PAGES_DEV))(jax.random.split(streams[4], N_RANK))
    column = jnp.arange(MAXP, dtype=jnp.int32)
    located = jnp.clip(starts[:, :, None] + column[None, None, :], 0, PAGES_DEV - 1)
    picked = jax.vmap(lambda table_row, spots: table_row[spots])(shuffle, located)
    tables = jnp.where(column[None, None, :] < counts[:, :, None], picked, 0)
    return (sizes_all.reshape(ROWS).astype(jnp.int32), tables.reshape(ROWS, MAXP).astype(jnp.int32))


def pool_normal(key):
    key = jax.random.fold_in(key, 21)
    return jnp.clip(jax.random.normal(key, (POOL, PAGE, LAT + ROPE), jnp.float32), -6.0, 6.0)


def draw_lengths(key, part):
    sizes_all, tables = slot_layout(key)
    return sizes_all


def draw_block_table(key, part):
    sizes_all, tables = slot_layout(key)
    return tables


def draw_cache_pool(key, part):
    values = pool_normal(key)
    return values.astype(jnp.bfloat16)


def draw_queries(key, part):
    key = jax.random.fold_in(key, 7)
    values = jnp.clip(jax.random.normal(key, (ROWS, H, LAT + ROPE), jnp.float32), -6.0, 6.0)
    return values.astype(jnp.bfloat16)


def steps_of(key, dims, cuts, smallest, high):
    loudness = 1.0
    for dim, shards_of in cuts:
        heights = jax.random.uniform(jax.random.fold_in(jax.random.fold_in(key, 6), dim), (shards_of,), jnp.float32, smallest / len(cuts), high / len(cuts))
        loudness = loudness * jnp.repeat(jnp.exp(heights), dims[dim] // shards_of).reshape((-1,) + (1,) * (len(dims) - 1 - dim))
    return loudness


def noise(key, dims, width, limit, cuts=(), kind=jnp.bfloat16):
    entries = jax.random.normal(key, dims, jnp.float32) * width
    if len(cuts) > 0:
        entries = steps_of(key, dims, cuts, -0.22, 0.18) * entries
    return jnp.clip(entries, min=-limit, max=limit).astype(kind)


def setup_inputs(seed: int = 0, part: int = 0) -> dict:
    keys = jax.random.split(jax.random.key(seed), 11)
    own_keys = jax.random.split(jax.random.fold_in(keys[10], part), 11)
    return {
        "queries": draw_queries(jax.random.fold_in(jax.random.fold_in(keys[10], part), 71), part),
        "cache_pool": draw_cache_pool(jax.random.fold_in(jax.random.fold_in(keys[10], part), 71), part),
        "lengths": draw_lengths(jax.random.fold_in(jax.random.fold_in(keys[10], part), 71), part),
        "block_table": draw_block_table(jax.random.fold_in(jax.random.fold_in(keys[10], part), 71), part),
        "residual": noise(own_keys[4], (ROWS, D), 0.5, 3.0, ((0, 32),)),
        "norm_gain": jnp.clip(1.0 + 0.18 * jax.random.normal(keys[5], (D,), jnp.float32), 0.099609375, 1.8984375).astype(jnp.bfloat16),
        "uv_weight": noise(keys[6], (H, LAT, HD), LAT ** -0.5, 0.25, ((0, 32),)),
        "out_weight": noise(keys[7], (H * HD, D), (H * HD) ** -0.5, 0.0625, ((1, 32),)),
        "gate_weight": noise(keys[8], (D, FF), D ** -0.5, 0.0625, ((1, 32),)),
        "up_weight": noise(keys[9], (D, FF), D ** -0.5, 0.0625, ((1, 32),)),
    }


score_scale = 192.0 ** (-0.5)

def norm_rows(mixed, norm_gain):
    values = mixed.astype(jnp.float32)
    factor = jax.lax.rsqrt(lax.optimization_barrier(jnp.mean(values * values, axis=-1, keepdims=True)) + 1e-06)
    return (values * factor * norm_gain.astype(jnp.float32)).astype(jnp.bfloat16)

def reference(queries, cache_pool, lengths, block_table, residual, norm_gain, uv_weight, out_weight, gate_weight, up_weight):
    owner = (jnp.arange(ROWS, dtype=jnp.int32) // R_DEV).astype(jnp.int32)
    pages = (block_table + owner[:, None] * PAGES_DEV).astype(jnp.int32)
    keys_all = cache_pool[pages].reshape(ROWS, MAXP * PAGE, LAT + ROPE).astype(jnp.float32)
    scores = jnp.einsum('rhc,rtc->rht', queries.astype(jnp.float32), keys_all) * score_scale
    position = jnp.arange(MAXP * PAGE, dtype=jnp.int32)
    valid = position[None, None, :] < lengths[:, None, None]
    scores = jnp.where(valid, scores, -1e+30)
    peak = lax.optimization_barrier(jnp.max(scores, axis=2, keepdims=True))
    expo = jnp.where(valid, jnp.exp(scores - peak), 0.0)
    total = lax.optimization_barrier(jnp.sum(expo, axis=2, keepdims=True))
    total = jnp.where(total > 0.0, total, 1.0)
    weights = (expo / total).astype(jnp.bfloat16)
    context = jnp.einsum('rht,rtc->rhc', weights.astype(jnp.float32), keys_all[:, :, :LAT]).astype(jnp.bfloat16)
    values = jnp.einsum('bhl,hld->bhd', context.astype(jnp.float32), uv_weight.astype(jnp.float32)).astype(jnp.bfloat16)
    attended = jnp.dot(values.reshape(ROWS, H * HD), out_weight, preferred_element_type=jnp.float32)
    mixed = (residual.astype(jnp.float32) + attended).astype(jnp.bfloat16)
    normed = norm_rows(mixed, norm_gain)
    gate = jnp.dot(normed, gate_weight, preferred_element_type=jnp.float32)
    upper = jnp.dot(normed, up_weight, preferred_element_type=jnp.float32)
    activ = (jax.nn.silu(gate) * upper).astype(jnp.bfloat16)
    return (mixed, activ)
```

```python
import jax
import jax.numpy as jnp
from jax import lax
from jax.experimental import pallas as pl
from jax.experimental.pallas import tpu as pltpu
from jax.sharding import PartitionSpec as P

F32 = jnp.float32
BF16 = jnp.bfloat16
MESH = pl.DeviceIdType.MESH

N = 32
SLOTS = 16
HEADS = 64
LAT = 512
WIDTH = 576
TOK = 512
PAGE = 32
MAXP = 4
D = 7168
COLS = 224
HID = 288
LANES = 256

NC = 2
SL = SLOTS // NC
RC = N * SL
HALF = RC // 2
SKEW = 8
STEPS = 33

score_scale = 192.0 ** (-0.5)


def kernel(
    len_ref, bt_ref, q_hbm, pool_hbm, res_hbm, gain_ref, uv_hbm, ow_hbm, gw_hbm, uw_hbm,
    mixed_ref, activ_ref,
    q_v, pool_v, res_v, uv_v, ow_v, gw_v, uw_v,
    mask_v, ctx, sbuf, cbuf, rs, rr, vbuf, mbuf, acc, accg, accu, ssq,
    load_sem, own_sem, res_send, res_recv, a2a_send, a2a_recv, ag_send, a_recv, b_recv, s_recv,
):
    me = lax.axis_index("rank")
    core = me % 2
    xx = (me // 2) % 4
    yy = me // 8
    sa = (1 - core) * 2 + core * 8
    sb = (1 - core) * 8 + core * 2
    a = (1 - core) * xx + core * yy
    b = (1 - core) * yy + core * xx
    sibling = me + 1 - 2 * core

    def rank_at(pa, pb):
        return pa * sa + pb * sb + core

    up_a, down_a = rank_at((a + 1) % 4, b), rank_at((a + 3) % 4, b)
    up_b, down_b = rank_at(a, (b + 1) % 4), rank_at(a, (b + 3) % 4)

    loads = [
        pltpu.make_async_copy(src, dst, load_sem.at[i])
        for i, (src, dst) in enumerate(
            [
                (q_hbm, q_v),
                (pool_hbm, pool_v),
                (res_hbm, res_v),
                (uv_hbm, uv_v),
                (ow_hbm, ow_v),
                (gw_hbm, gw_v.at[pl.ds(0, D)]),
                (uw_hbm, uw_v.at[pl.ds(0, D)]),
            ]
        )
    ]
    for load in loads:
        load.start()

    barrier = pltpu.get_barrier_semaphore()

    def greet(k, carry):
        pl.semaphore_signal(barrier, inc=1, device_id={"rank": (me + k) % N}, device_id_type=MESH)
        return carry

    lax.fori_loop(1, N, greet, 0)

    lane = lax.broadcasted_iota(jnp.int32, (1, TOK), 1)
    page_of = lane // PAGE
    offset = lane % PAGE
    for slot in range(SLOTS):
        n = len_ref[slot]
        valid = jnp.zeros((1, TOK), F32)
        for m in range(MAXP):
            hit = (page_of == bt_ref[slot, m]) & (offset + m * PAGE < n)
            valid = jnp.where(hit, 1.0, valid)
        mask_v[slot // 4, slot % 4 : slot % 4 + 1, :] = valid
    gw_v[D:, :] = jnp.zeros((32, HID), BF16)
    uw_v[D:, :] = jnp.zeros((32, HID), BF16)
    acc[...] = jnp.zeros_like(acc)
    accg[...] = jnp.zeros_like(accg)
    accu[...] = jnp.zeros_like(accu)
    ssq[...] = jnp.zeros_like(ssq)

    loads[2].wait()
    for r in range(N):
        rs[r, :, 0:COLS] = res_v[:, r * COLS : (r + 1) * COLS]
        rs[r, :, COLS:LANES] = jnp.zeros((SLOTS, LANES - COLS), BF16)
    loads[0].wait()
    loads[1].wait()

    pl.semaphore_wait(barrier, N - 1)

    def dest_of(k):
        p = (k * 11) % N
        return ((yy + p // 8) % 4) * 8 + ((xx + (p // 2) % 4) % 4) * 2 + (core + p % 2) % 2

    def send_res(k, carry):
        to = dest_of(k)
        pltpu.make_async_remote_copy(
            src_ref=rs.at[to], dst_ref=rr.at[me], send_sem=res_send, recv_sem=res_recv,
            device_id={"rank": to}, device_id_type=MESH,
        ).start()
        return carry

    lax.fori_loop(1, N, send_res, 0)
    own_res = pltpu.make_async_copy(rs.at[me], rr.at[me], own_sem.at[NC])
    own_res.start()

    def attend(first, carry):
        q = q_v[pl.ds(first * 4, 4)].reshape(4 * HEADS, WIDTH)
        scores = lax.dot_general(
            q, pool_v[...].reshape(TOK, WIDTH), (((1,), (1,)), ((), ())), preferred_element_type=F32
        ) * score_scale
        ok = jnp.broadcast_to(
            mask_v[first][:, None, :], (4, HEADS, TOK)
        ).reshape(4 * HEADS, TOK) > 0.0
        scores = jnp.where(ok, scores, -1e30)
        peak = jnp.max(scores, axis=1, keepdims=True)
        expo = jnp.where(ok, jnp.exp(scores - peak), 0.0)
        total = jnp.sum(expo, axis=1, keepdims=True)
        total = jnp.where(total > 0.0, total, 1.0)
        weights = (expo / total).astype(BF16)
        out = jnp.dot(weights, pool_v[...].reshape(TOK, WIDTH)[:, :LAT], preferred_element_type=F32)
        for part in range(LAT // 128):
            ctx[part, pl.ds(pl.multiple_of(first * 4 * HEADS, 4 * HEADS), 4 * HEADS), :] = out[
                :, part * 128 : (part + 1) * 128
            ]
        return carry

    own_ctx = []
    for ch in range(NC):
        lax.fori_loop(ch * SL // 4, (ch + 1) * SL // 4, attend, 0)

        def pack(r, carry, ch=ch):
            for part in range(LAT // 128):
                pair = [
                    ctx[part, pl.ds(ch * SL * HEADS + 2 * r + h, SL, stride=HEADS), :] for h in range(2)
                ]
                sbuf[ch, r, :, part * 128 : (part + 1) * 128] = jnp.concatenate(pair, axis=0).astype(BF16)
            return carry

        lax.fori_loop(0, N, pack, 0)

        def send_ctx(k, carry, ch=ch):
            to = dest_of(k)
            pltpu.make_async_remote_copy(
                src_ref=sbuf.at[ch, to], dst_ref=cbuf.at[ch, me],
                send_sem=a2a_send.at[ch], recv_sem=a2a_recv.at[ch],
                device_id={"rank": to}, device_id_type=MESH,
            ).start()
            return carry

        lax.fori_loop(1, N, send_ctx, 0)
        own_ctx.append(pltpu.make_async_copy(sbuf.at[ch, me], cbuf.at[ch, me], own_sem.at[ch]))
        own_ctx[ch].start()

    for load in loads[3:]:
        load.wait()
    own_res.wait()
    pltpu.make_async_remote_copy(
        src_ref=rs.at[pl.ds(0, N - 1)], dst_ref=rr.at[pl.ds(0, N - 1)], send_sem=res_send, recv_sem=res_recv,
        device_id={"rank": sibling}, device_id_type=MESH,
    ).wait()

    def turn(j):
        return (4 - j + (j // 2) * 3 + (j // 3) * 2) % 4

    def place(k):
        middle = (k // 4 + 1) // 2 - 2 * (k // 12)
        last = k // 12
        j = (1 - middle) * (k % 4) + middle * (((k + 12) % 16) // 2)
        i = middle * (1 + k % 2) + last * 3
        return j, i

    def shard(k):
        j, i = place(k)
        return rank_at((a + turn(j)) % 4, (b + turn(i)) % 4)

    def other_shard(k):
        j, i = place(k)
        return ((b + turn(j)) % 4) * sb + ((a + turn(i)) % 4) * sa + (1 - core)

    def action(g, ch, k, buf):
        s = shard(k)
        j, i = place(k)
        full = buf.at[ch, s]
        top = buf.at[ch, s, pl.ds(0, HALF)]
        bottom = buf.at[ch, s, pl.ds(HALF, HALF)]

        def push(ref, sem, to):
            pltpu.make_async_remote_copy(
                src_ref=ref, dst_ref=ref, send_sem=ag_send.at[g, ch], recv_sem=sem,
                device_id={"rank": to}, device_id_type=MESH,
            ).start()

        def arrive(ref, sem):
            pltpu.make_async_remote_copy(
                src_ref=ref, dst_ref=ref, send_sem=ag_send.at[g, ch], recv_sem=sem,
                device_id={"rank": sibling}, device_id_type=MESH,
            ).wait_recv()

        @pl.when(k == 0)
        def _():
            push(full, a_recv.at[g, ch, 0], up_a)
            push(full, a_recv.at[g, ch, 1], down_a)

        @pl.when(k == 1)
        def _():
            arrive(full, a_recv.at[g, ch, 0])
            push(top, a_recv.at[g, ch, 2], up_a)

        @pl.when(k == 2)
        def _():
            arrive(full, a_recv.at[g, ch, 1])
            push(bottom, a_recv.at[g, ch, 3], down_a)

        @pl.when(k == 3)
        def _():
            arrive(top, a_recv.at[g, ch, 2])
            arrive(bottom, a_recv.at[g, ch, 3])

        @pl.when(k < 4)
        def _():
            push(full, b_recv.at[g, ch, j * 4], up_b)
            push(full, b_recv.at[g, ch, j * 4 + 1], down_b)

        @pl.when((k >= 4) & (k < 12) & (k % 2 == 0))
        def _():
            arrive(full, b_recv.at[g, ch, j * 4])
            push(top, b_recv.at[g, ch, j * 4 + 2], up_b)

        @pl.when((k >= 4) & (k < 12) & (k % 2 == 1))
        def _():
            arrive(full, b_recv.at[g, ch, j * 4 + 1])
            push(bottom, b_recv.at[g, ch, j * 4 + 3], down_b)

        @pl.when(k >= 12)
        def _():
            arrive(top, b_recv.at[g, ch, j * 4 + 2])
            arrive(bottom, b_recv.at[g, ch, j * 4 + 3])

        push(full, s_recv.at[g, ch, k], sibling)

    def arrive_other(g, ch, k, buf):
        ref = buf.at[ch, other_shard(k)]
        pltpu.make_async_remote_copy(
            src_ref=ref, dst_ref=ref, send_sem=ag_send.at[g, ch], recv_sem=s_recv.at[g, ch, k],
            device_id={"rank": sibling}, device_id_type=MESH,
        ).wait_recv()

    def out_part(ch, s):
        w = ow_v[pl.ds(pl.multiple_of(s * LANES, LANES), LANES), :]
        return jnp.dot(vbuf[ch, s], w, preferred_element_type=F32)

    def hidden_part(ch, s):
        x = mbuf[ch, s].astype(F32)
        squares = x * x
        ssq[ch] += squares[:, :128] + squares[:, 128:]
        xg = (x * gain_ref[pl.ds(s, 1), :]).astype(BF16)
        rows = pl.ds(pl.multiple_of(s * COLS, 32), LANES)
        accg[ch] += jnp.dot(xg, gw_v[rows, :], preferred_element_type=F32)
        accu[ch] += jnp.dot(xg, uw_v[rows, :], preferred_element_type=F32)

    def step(u, ch):
        @pl.when(u == 0)
        def _():
            own_ctx[ch].wait()
            pltpu.make_async_remote_copy(
                src_ref=sbuf.at[ch, pl.ds(0, N - 1)], dst_ref=cbuf.at[ch, pl.ds(0, N - 1)],
                send_sem=a2a_send.at[ch], recv_sem=a2a_recv.at[ch],
                device_id={"rank": sibling}, device_id_type=MESH,
            ).wait_recv()
            uv = jnp.concatenate([uv_v[0], uv_v[1]], axis=1)
            z = jnp.dot(cbuf[ch].reshape(N * 2 * SL, LAT), uv, preferred_element_type=F32)
            z = z.reshape(N, 2, SL, LANES)
            first = z[:, 0, :, :128].reshape(RC, 128)
            second = z[:, 1, :, 128:].reshape(RC, 128)
            vbuf[ch, me] = jnp.concatenate([first, second], axis=1).astype(BF16)

        @pl.when((u >= 0) & (u < 16))
        def _():
            action(0, ch, u, vbuf)

        @pl.when((u >= 1) & (u <= 16))
        def _():
            arrive_other(0, ch, u - 1, vbuf)
            acc[ch] += out_part(ch, shard(u - 1)) + out_part(ch, other_shard(u - 1))

        @pl.when(u == 16)
        def _():
            res = rr[...].astype(F32)[:, ch * SL : (ch + 1) * SL, :].reshape(RC, LANES)
            mbuf[ch, me] = jnp.zeros((RC, LANES), BF16)
            mbuf[ch, me, :, 0:COLS] = (res[:, 0:COLS] + acc[ch]).astype(BF16)

        @pl.when((u >= 16) & (u < 32))
        def _():
            action(1, ch, u - 16, mbuf)

        @pl.when((u >= 17) & (u <= 32))
        def _():
            arrive_other(1, ch, u - 17, mbuf)
            hidden_part(ch, shard(u - 17))
            hidden_part(ch, other_shard(u - 17))

    def body(t, carry):
        for ch in range(NC):
            step(t - ch * SKEW, ch)
        return carry

    lax.fori_loop(0, STEPS + (NC - 1) * SKEW, body, 0)

    pair = pl.ds(pl.multiple_of((me // 2) * 16, 16), 16)
    odd = core > 0
    for s in range(N):
        both = []
        for ch in range(NC):
            tile = mbuf[ch, s, pair, :].astype(F32)
            both.append(jnp.where(odd, tile[8:], tile[:8]))
        mixed_ref[:, s * COLS : (s + 1) * COLS] = jnp.concatenate(both, axis=0)[:, :COLS].astype(BF16)

    pieces = []
    for ch in range(NC):
        factor = lax.rsqrt(jnp.sum(ssq[ch], axis=1, keepdims=True) * (1.0 / D) + 1e-6)
        gate = accg[ch] * factor
        upper = accu[ch] * factor
        pieces.append((gate / (1.0 + jnp.exp(-gate)) * upper).reshape(N, SL, HID))
    activ_ref[...] = jnp.concatenate(pieces, axis=1).reshape(N * SLOTS, HID).astype(BF16)

    def sent(buf, sem):
        pltpu.make_async_remote_copy(
            src_ref=buf.at[pl.ds(0, N - 1)], dst_ref=buf.at[pl.ds(0, N - 1)], send_sem=sem, recv_sem=res_recv,
            device_id={"rank": sibling}, device_id_type=MESH,
        ).wait_send()

    for ch in range(NC):
        sent(sbuf.at[ch], a2a_send.at[ch])
        sent(vbuf.at[ch], ag_send.at[0, ch])
        sent(mbuf.at[ch], ag_send.at[1, ch])


def per_device(
    queries, cache_pool, lengths, block_table, residual, norm_gain, uv_weight, out_weight, gate_weight, up_weight
):
    gain = jnp.pad(norm_gain.reshape(N, COLS).astype(F32), ((0, 0), (0, LANES - COLS)))
    vmem = pl.BlockSpec(memory_space=pltpu.VMEM)
    smem = pl.BlockSpec(memory_space=pltpu.SMEM)
    hbm = pl.BlockSpec(memory_space=pl.ANY)
    dma = pltpu.SemaphoreType.DMA
    return pl.pallas_call(
        kernel,
        out_shape=(
            jax.ShapeDtypeStruct((SLOTS, D), BF16),
            jax.ShapeDtypeStruct((N * SLOTS, HID), BF16),
        ),
        in_specs=[smem, smem, hbm, hbm, hbm, vmem, hbm, hbm, hbm, hbm],
        out_specs=(vmem, vmem),
        scratch_shapes=[
            pltpu.VMEM((SLOTS, HEADS, WIDTH), BF16),
            pltpu.VMEM((SLOTS, PAGE, WIDTH), BF16),
            pltpu.VMEM((SLOTS, D), BF16),
            pltpu.VMEM((2, LAT, 128), BF16),
            pltpu.VMEM((N * LANES, COLS), BF16),
            pltpu.VMEM((D + 32, HID), BF16),
            pltpu.VMEM((D + 32, HID), BF16),
            pltpu.VMEM((SLOTS // 4, 4, TOK), F32),
            pltpu.VMEM((LAT // 128, SLOTS * HEADS, 128), F32),
            pltpu.VMEM((NC, N, 2 * SL, LAT), BF16),
            pltpu.VMEM((NC, N, 2 * SL, LAT), BF16),
            pltpu.VMEM((N, SLOTS, LANES), BF16),
            pltpu.VMEM((N, SLOTS, LANES), BF16),
            pltpu.VMEM((NC, N, RC, LANES), BF16),
            pltpu.VMEM((NC, N, RC, LANES), BF16),
            pltpu.VMEM((NC, RC, COLS), F32),
            pltpu.VMEM((NC, RC, HID), F32),
            pltpu.VMEM((NC, RC, HID), F32),
            pltpu.VMEM((NC, RC, 128), F32),
            dma((7,)),
            dma((NC + 1,)),
            dma,
            dma,
            dma((NC,)),
            dma((NC,)),
            dma((2, NC)),
            dma((2, NC, 4)),
            dma((2, NC, 16)),
            dma((2, NC, 16)),
        ],
        compiler_params=pltpu.CompilerParams(
            collective_id=0, has_side_effects=True, vmem_limit_bytes=60 * 1024 * 1024
        ),
        cost_estimate=pl.CostEstimate(flops=7 * 10**9, bytes_accessed=15 * 10**6, transcendentals=10**6),
    )(
        lengths, block_table, queries, cache_pool, residual, gain, uv_weight, out_weight, gate_weight, up_weight
    )


def solution(mesh):
    placed = (
        P(("group", "rank"), None, None),
        P(("group", "rank"), None, None),
        P(("group", "rank")),
        P(("group", "rank"), None),
        P(("group", "rank"), None),
        P(),
        P("rank", None, None),
        P(None, "rank"),
        P(None, "rank"),
        P(None, "rank"),
    )
    return jax.shard_map(
        per_device,
        mesh=mesh,
        in_specs=placed,
        out_specs=(P(("group", "rank"), None), P("group", "rank")),
        check_vma=False,
    )
```

```python
import jax
import jax.numpy as jnp
from jax import lax
from jax.experimental import pallas as pl
from jax.experimental.pallas import tpu as pltpu
from jax.sharding import PartitionSpec as P

F32 = jnp.float32
BF16 = jnp.bfloat16
MESH = pl.DeviceIdType.MESH

N = 32
SLOTS = 16
HEADS = 64
LAT = 512
WIDTH = 576
TOK = 512
PAGE = 32
MAXP = 4
D = 7168
COLS = 224
HID = 288
LANES = 256

NC = 2
SL = SLOTS // NC
RC = N * SL

FULL, TOP, BOTTOM = range(3)

score_scale = 192.0 ** (-0.5)


def kernel(
    len_ref, bt_ref, q_hbm, pool_hbm, res_hbm, gain_hbm, uv_hbm, ow_hbm, gw_hbm, uw_hbm,
    mixed_ref, activ_ref,
    q_v, pool_v, res_v, uv_v, ow_v, gw_v, uw_v,
    gain_v, gain_w, mask_v, ctx, sbuf, cbuf, rs, rr, vbuf, mbuf, wp, acc, hid, ssq, picked, own_rows, order, out,
    load_sem, own_sem, res_send, res_recv, a2a_send, a2a_recv, ag_send, a_recv, b_recv, s_recv,
):
    me = lax.axis_index("rank")
    core = me % 2
    xx = (me // 2) % 4
    yy = me // 8
    sa = (1 - core) * 2 + core * 8
    sb = (1 - core) * 8 + core * 2
    a = (1 - core) * xx + core * yy
    b = (1 - core) * yy + core * xx
    sibling = me + 1 - 2 * core

    def rank_at(pa, pb):
        return pa * sa + pb * sb + core

    up_a, down_a = rank_at((a + 1) % 4, b), rank_at((a + 3) % 4, b)
    up_b, down_b = rank_at(a, (b + 1) % 4), rank_at(a, (b + 3) % 4)

    barrier = pltpu.get_barrier_semaphore()

    def greet(k, carry):
        pl.semaphore_signal(barrier, inc=1, device_id={"rank": (me + k) % N}, device_id_type=MESH)
        return carry

    lax.fori_loop(1, N, greet, 0)

    loads = [
        pltpu.make_async_copy(src, dst, load_sem.at[i])
        for i, (src, dst) in enumerate(
            [
                (q_hbm, q_v),
                (pool_hbm, pool_v),
                (res_hbm, res_v),
                (uv_hbm, uv_v),
                (ow_hbm, ow_v),
                (gw_hbm, gw_v),
                (uw_hbm, uw_v),
                (gain_hbm, gain_v),
            ]
        )
    ]
    for load in loads:
        load.start()

    lane = lax.broadcasted_iota(jnp.int32, (1, TOK), 1)
    page_of = lane // PAGE
    offset = lane % PAGE
    for slot in range(SLOTS):
        n = len_ref[slot]
        valid = jnp.zeros((1, TOK), F32)
        for m in range(MAXP):
            hit = (page_of == bt_ref[m, slot]) & (offset + m * PAGE < n)
            valid = jnp.where(hit, 1.0, valid)
        mask_v[slot // 4, slot % 4 : slot % 4 + 1, :] = valid
    hid[...] = jnp.zeros_like(hid)
    ssq[...] = jnp.zeros_like(ssq)
    row = lax.broadcasted_iota(jnp.int32, (NC * RC, NC * RC), 0)
    col = lax.broadcasted_iota(jnp.int32, (NC * RC, NC * RC), 1)
    home = (row % RC) // SL * SLOTS + row // RC * SL + row % SL
    order[...] = jnp.where(home == col, 1.0, 0.0).astype(BF16)
    for ch in range(NC):
        slot = lax.broadcasted_iota(jnp.int32, (SLOTS, RC), 0)
        col = lax.broadcasted_iota(jnp.int32, (SLOTS, RC), 1)
        hit = (slot // SL == ch) & (col == me * SL + slot % SL)
        own_rows[ch] = jnp.where(hit, 1.0, 0.0).astype(BF16)

    loads[0].wait()
    loads[1].wait()

    def dest_of(k):
        p = (k * 11) % N
        return ((yy + p // 8) % 4) * 8 + ((xx + (p // 2) % 4) % 4) * 2 + (core + p % 2) % 2

    def attend(first, carry):
        q = q_v[pl.ds(first * 4, 4)].reshape(4 * HEADS, WIDTH)
        scores = lax.dot_general(
            q, pool_v[...].reshape(TOK, WIDTH), (((1,), (1,)), ((), ())), preferred_element_type=F32
        ) * score_scale
        ok = jnp.broadcast_to(
            mask_v[first][:, None, :], (4, HEADS, TOK)
        ).reshape(4 * HEADS, TOK) > 0.0
        scores = jnp.where(ok, scores, -1e30)
        peak = jnp.max(scores, axis=1, keepdims=True)
        expo = jnp.where(ok, jnp.exp(scores - peak), 0.0)
        total = jnp.sum(expo, axis=1, keepdims=True)
        total = jnp.where(total > 0.0, total, 1.0)
        weights = (expo / total).astype(BF16)
        out = jnp.dot(weights, pool_v[...].reshape(TOK, WIDTH)[:, :LAT], preferred_element_type=F32)
        for part in range(LAT // 128):
            ctx[part, pl.ds(pl.multiple_of(first * 4 * HEADS, 4 * HEADS), 4 * HEADS), :] = out[
                :, part * 128 : (part + 1) * 128
            ]
        return carry

    own_ctx = []
    for ch in range(NC):
        lax.fori_loop(ch * SL // 4, (ch + 1) * SL // 4, attend, 0)

        def pack(r, carry, ch=ch):
            for part in range(LAT // 128):
                pair = [
                    ctx[part, pl.ds(ch * SL * HEADS + 2 * r + h, SL, stride=HEADS), :] for h in range(2)
                ]
                sbuf[ch, r, :, part * 128 : (part + 1) * 128] = jnp.concatenate(pair, axis=0).astype(BF16)
            return carry

        lax.fori_loop(0, N, pack, 0)

        if ch == 0:
            pl.semaphore_wait(barrier, N - 1)

        def send_ctx(k, carry, ch=ch):
            to = dest_of(k)
            pltpu.make_async_remote_copy(
                src_ref=sbuf.at[ch, to], dst_ref=cbuf.at[ch, me],
                send_sem=a2a_send.at[ch], recv_sem=a2a_recv.at[ch],
                device_id={"rank": to}, device_id_type=MESH,
            ).start()
            return carry

        lax.fori_loop(1, N, send_ctx, 0)
        own_ctx.append(pltpu.make_async_copy(sbuf.at[ch, me], cbuf.at[ch, me], own_sem.at[ch]))
        own_ctx[ch].start()

    loads[2].wait()
    for r in range(N):
        rs[r, :, 0:COLS] = res_v[:, r * COLS : (r + 1) * COLS]
        rs[r, :, COLS:LANES] = jnp.zeros((SLOTS, LANES - COLS), BF16)

    def send_res(k, carry):
        to = dest_of(k)
        pltpu.make_async_remote_copy(
            src_ref=rs.at[to], dst_ref=rr.at[me], send_sem=res_send, recv_sem=res_recv,
            device_id={"rank": to}, device_id_type=MESH,
        ).start()
        return carry

    lax.fori_loop(1, N, send_res, 0)
    own_res = pltpu.make_async_copy(rs.at[me], rr.at[me], own_sem.at[NC])
    own_res.start()

    for load in loads[3:]:
        load.wait()

    gain_w[...] = gain_v[...].astype(F32)

    def align(q, carry):
        lanes = pl.ds(pl.multiple_of(q * 4 * COLS, 128), 4 * COLS)
        gain = jnp.concatenate([gain_w[pl.ds(q * 7 + i, 1), :] for i in range(7)], axis=1)
        for first, w in ((0, gw_v), (HID, uw_v)):
            scaled = (w[:, lanes].astype(F32) * gain).astype(BF16)
            for i in range(4):
                wp[q * 4 + i, first : first + HID, :] = scaled[:, i * COLS : (i + 1) * COLS]
        return carry

    lax.fori_loop(0, N // 4, align, 0)

    def turn(j):
        return (4 - j + (j // 2) * 3 + (j // 3) * 2) % 4

    def shard(j, i):
        return rank_at((a + turn(j)) % 4, (b + turn(i)) % 4)

    def other_shard(j, i):
        return ((b + turn(j)) % 4) * sb + ((a + turn(i)) % 4) * sa + (1 - core)

    bufs = (vbuf, mbuf)

    def piece(g, ch, s, part):
        buf = bufs[g]
        half = buf.shape[2] // 2
        if part == FULL:
            return buf.at[ch, s]
        return buf.at[ch, s, pl.ds(0 if part == TOP else half, half)]

    def push(g, ch, ref, sem, to):
        pltpu.make_async_remote_copy(
            src_ref=ref, dst_ref=ref, send_sem=ag_send.at[g, ch], recv_sem=sem,
            device_id={"rank": to}, device_id_type=MESH,
        ).start()

    def arrive(g, ch, ref, sem):
        pltpu.make_async_remote_copy(
            src_ref=ref, dst_ref=ref, send_sem=ag_send.at[g, ch], recv_sem=sem,
            device_id={"rank": sibling}, device_id_type=MESH,
        ).wait_recv()

    def share(g, ch, j, i):
        push(g, ch, piece(g, ch, shard(j, i), FULL), s_recv.at[g, ch, j * 4 + i], sibling)

    def along_b(g, ch, j):
        full = piece(g, ch, shard(j, 0), FULL)
        push(g, ch, full, b_recv.at[g, ch, j * 4], up_b)
        push(g, ch, full, b_recv.at[g, ch, j * 4 + 1], down_b)
        share(g, ch, j, 0)

    def open_line(g, ch):
        own = piece(g, ch, me, FULL)
        push(g, ch, own, a_recv.at[g, ch, 0], up_a)
        push(g, ch, own, a_recv.at[g, ch, 1], down_a)
        along_b(g, ch, 0)

    def own_line(g, ch):
        s = shard(1, 0)
        arrive(g, ch, piece(g, ch, s, FULL), a_recv.at[g, ch, 0])
        push(g, ch, piece(g, ch, s, TOP), a_recv.at[g, ch, 2], up_a)
        along_b(g, ch, 1)
        s = shard(2, 0)
        arrive(g, ch, piece(g, ch, s, FULL), a_recv.at[g, ch, 1])
        push(g, ch, piece(g, ch, s, BOTTOM), a_recv.at[g, ch, 3], down_a)
        along_b(g, ch, 2)
        s = shard(3, 0)
        arrive(g, ch, piece(g, ch, s, TOP), a_recv.at[g, ch, 2])
        arrive(g, ch, piece(g, ch, s, BOTTOM), a_recv.at[g, ch, 3])
        along_b(g, ch, 3)

    def next_lines(g, ch, j):
        s = shard(j, 1)
        arrive(g, ch, piece(g, ch, s, FULL), b_recv.at[g, ch, j * 4])
        push(g, ch, piece(g, ch, s, TOP), b_recv.at[g, ch, j * 4 + 2], up_b)
        share(g, ch, j, 1)
        s = shard(j, 2)
        arrive(g, ch, piece(g, ch, s, FULL), b_recv.at[g, ch, j * 4 + 1])
        push(g, ch, piece(g, ch, s, BOTTOM), b_recv.at[g, ch, j * 4 + 3], down_b)
        share(g, ch, j, 2)

    def last_line(g, ch, j):
        s = shard(j, 3)
        arrive(g, ch, piece(g, ch, s, TOP), b_recv.at[g, ch, j * 4 + 2])
        arrive(g, ch, piece(g, ch, s, BOTTOM), b_recv.at[g, ch, j * 4 + 3])
        share(g, ch, j, 3)

    def out_part(ch, s):
        w = ow_v[:, pl.ds(pl.multiple_of(s * LANES, LANES), LANES)]
        return lax.dot_general(w, vbuf[ch, s], (((1,), (1,)), ((), ())), preferred_element_type=F32)

    def hidden_part(ch, s):
        x = mbuf[ch, s]
        wide = x.astype(F32)
        ssq[ch] += jnp.sum((wide * wide).reshape(COLS // 8, 8, RC), axis=0)
        picked[ch, s] = lax.dot_general(own_rows[ch], x, (((1,), (1,)), ((), ())), preferred_element_type=F32)
        return jnp.dot(wp[s], x, preferred_element_type=F32)

    def compute(g, ch, j, lines):
        total, part = ((acc, out_part), (hid, hidden_part))[g]
        for i in lines:
            arrive(g, ch, piece(g, ch, other_shard(j, i), FULL), s_recv.at[g, ch, j * 4 + i])
        total[ch] += sum(part(ch, s(j, i)) for i in lines for s in (shard, other_shard))

    def item(n):
        ch = (n + 3) // 8 + (n + 7) // 8 - (n + 6) // 8
        j = ((n + 6) // 8) * (n - 1) - 3 * ((n + 3) // 8)
        return ch, j

    def gather(g, finish):
        for ch in range(NC):
            own_line(g, ch)

        def middle(n, carry):
            next_lines(g, *item(n))
            compute(g, *item(n), (0,))

            @pl.when(n > 0)
            def _():
                compute(g, *item(n - 1), (1, 2))

            return carry

        lax.fori_loop(0, 8, middle, 0)
        last_line(g, *item(0))
        compute(g, *item(7), (1, 2))

        def ending(n, carry):
            last_line(g, *item(n))
            compute(g, *item(n - 1), (3,))
            return carry

        lax.fori_loop(1, 5, ending, 0)
        compute(g, *item(4), (3,))
        finish(0)
        last_line(g, *item(5))
        lax.fori_loop(6, 8, ending, 0)
        compute(g, *item(7), (3,))
        finish(1)

    for ch in range(NC):
        own_ctx[ch].wait()
        pltpu.make_async_remote_copy(
            src_ref=sbuf.at[ch, pl.ds(0, N - 1)], dst_ref=cbuf.at[ch, pl.ds(0, N - 1)],
            send_sem=a2a_send.at[ch], recv_sem=a2a_recv.at[ch],
            device_id={"rank": sibling}, device_id_type=MESH,
        ).wait_recv()
        uv = jnp.concatenate([uv_v[0], uv_v[1]], axis=1)
        z = jnp.dot(cbuf[ch].reshape(N * 2 * SL, LAT), uv, preferred_element_type=F32)
        z = z.reshape(N, 2, SL, LANES)
        first = z[:, 0, :, :128].reshape(RC, 128)
        second = z[:, 1, :, 128:].reshape(RC, 128)
        vbuf[ch, me] = jnp.concatenate([first, second], axis=1).astype(BF16)
        open_line(0, ch)

    own_res.wait()
    pltpu.make_async_remote_copy(
        src_ref=rs.at[pl.ds(0, N - 1)], dst_ref=rr.at[pl.ds(0, N - 1)], send_sem=res_send, recv_sem=res_recv,
        device_id={"rank": sibling}, device_id_type=MESH,
    ).wait()
    for ch in range(NC):
        res = rr[...].astype(F32)[:, ch * SL : (ch + 1) * SL, :].reshape(RC, LANES)
        acc[ch] = res.T[:COLS]

    def mix(ch):
        mbuf[ch, me] = acc[ch].astype(BF16)
        open_line(1, ch)

    def finish(ch):
        factor = lax.rsqrt(jnp.sum(ssq[ch], axis=0, keepdims=True) * (1.0 / D) + 1e-6)
        gate = hid[ch, :HID] * factor
        upper = hid[ch, HID:] * factor
        activ = (gate / (1.0 + jnp.exp(-gate)) * upper).astype(BF16)
        out[ch] = jnp.dot(activ, order[ch * RC : (ch + 1) * RC, :], preferred_element_type=F32)

    gather(0, mix)
    gather(1, finish)

    for s in range(N):
        rows = picked[0, s]
        for ch in range(1, NC):
            rows += picked[ch, s]
        mixed_ref[:, s * COLS : (s + 1) * COLS] = rows.astype(BF16)

    activ_ref[...] = (out[0] + out[1]).astype(BF16)

    def sent(buf, sem):
        pltpu.make_async_remote_copy(
            src_ref=buf.at[pl.ds(0, N - 1)], dst_ref=buf.at[pl.ds(0, N - 1)], send_sem=sem, recv_sem=res_recv,
            device_id={"rank": sibling}, device_id_type=MESH,
        ).wait_send()

    for ch in range(NC):
        sent(sbuf.at[ch], a2a_send.at[ch])
        sent(vbuf.at[ch], ag_send.at[0, ch])
        sent(mbuf.at[ch], ag_send.at[1, ch])


def hand_out(mixed_in, activ_in, mixed_out, activ_out, sem):
    copies = [
        pltpu.make_async_copy(mixed_in, mixed_out, sem.at[0]),
        pltpu.make_async_copy(activ_in, activ_out, sem.at[1]),
    ]
    for copy in copies:
        copy.start()
    for copy in copies:
        copy.wait()


def per_device(
    queries, cache_pool, lengths, block_table, residual, norm_gain, uv_weight, out_weight, gate_weight, up_weight
):
    gain = norm_gain.reshape(D // 128, 128)
    vmem = pl.BlockSpec(memory_space=pltpu.VMEM)
    smem = pl.BlockSpec(memory_space=pltpu.SMEM)
    hbm = pl.BlockSpec(memory_space=pl.ANY)
    dma = pltpu.SemaphoreType.DMA
    mixed, activ = pl.pallas_call(
        kernel,
        out_shape=(
            jax.ShapeDtypeStruct((SLOTS, D), BF16),
            jax.ShapeDtypeStruct((HID, N * SLOTS), BF16),
        ),
        in_specs=[smem, smem] + [hbm] * 8,
        out_specs=(vmem, vmem),
        scratch_shapes=[
            pltpu.VMEM((SLOTS, HEADS, WIDTH), BF16),
            pltpu.VMEM((SLOTS, PAGE, WIDTH), BF16),
            pltpu.VMEM((SLOTS, D), BF16),
            pltpu.VMEM((2, LAT, 128), BF16),
            pltpu.VMEM((COLS, N * LANES), BF16),
            pltpu.VMEM((HID, D), BF16),
            pltpu.VMEM((HID, D), BF16),
            pltpu.VMEM((D // 128, 128), BF16),
            pltpu.VMEM((D // 128, 128), F32),
            pltpu.VMEM((SLOTS // 4, 4, TOK), F32),
            pltpu.VMEM((LAT // 128, SLOTS * HEADS, 128), F32),
            pltpu.VMEM((NC, N, 2 * SL, LAT), BF16),
            pltpu.VMEM((NC, N, 2 * SL, LAT), BF16),
            pltpu.VMEM((N, SLOTS, LANES), BF16),
            pltpu.VMEM((N, SLOTS, LANES), BF16),
            pltpu.VMEM((NC, N, RC, LANES), BF16),
            pltpu.VMEM((NC, N, COLS, RC), BF16),
            pltpu.VMEM((N, 2 * HID, COLS), BF16),
            pltpu.VMEM((NC, COLS, RC), F32),
            pltpu.VMEM((NC, 2 * HID, RC), F32),
            pltpu.VMEM((NC, 8, RC), F32),
            pltpu.VMEM((NC, N, SLOTS, COLS), F32),
            pltpu.VMEM((NC, SLOTS, RC), BF16),
            pltpu.VMEM((NC * RC, NC * RC), BF16),
            pltpu.VMEM((NC, HID, NC * RC), F32),
            dma((8,)),
            dma((NC + 1,)),
            dma,
            dma,
            dma((NC,)),
            dma((NC,)),
            dma((2, NC)),
            dma((2, NC, 4)),
            dma((2, NC, 16)),
            dma((2, NC, 16)),
        ],
        compiler_params=pltpu.CompilerParams(
            collective_id=0, has_side_effects=True, vmem_limit_bytes=60 * 1024 * 1024
        ),
        cost_estimate=pl.CostEstimate(flops=7 * 10**9, bytes_accessed=15 * 10**6, transcendentals=10**6),
    )(
        lengths, block_table.T, queries, cache_pool, residual, gain, uv_weight,
        out_weight.T, gate_weight.T, up_weight.T,
    )
    mixed, activ = pl.pallas_call(
        hand_out,
        out_shape=(
            jax.ShapeDtypeStruct((SLOTS, D), BF16),
            jax.ShapeDtypeStruct((HID, N * SLOTS), BF16),
        ),
        in_specs=[vmem, vmem],
        out_specs=(hbm, hbm),
        scratch_shapes=[dma((2,))],
    )(mixed, activ)
    return mixed, activ.T


def solution(mesh):
    placed = (
        P(("group", "rank"), None, None),
        P(("group", "rank"), None, None),
        P(("group", "rank")),
        P(("group", "rank"), None),
        P(("group", "rank"), None),
        P(),
        P("rank", None, None),
        P(None, "rank"),
        P(None, "rank"),
        P(None, "rank"),
    )
    return jax.shard_map(
        per_device,
        mesh=mesh,
        in_specs=placed,
        out_specs=(P(("group", "rank"), None), P("group", "rank")),
        check_vma=False,
    )
```

```python
import jax
import jax.numpy as jnp
from jax import lax
from jax.experimental import pallas as pl
from jax.experimental.pallas import tpu as pltpu
from jax.sharding import PartitionSpec as P

F32 = jnp.float32
BF16 = jnp.bfloat16
MESH = pl.DeviceIdType.MESH

N = 32
SLOTS = 16
HEADS = 64
LAT = 512
WIDTH = 576
TOK = 512
PAGE = 32
MAXP = 4
D = 7168
COLS = 224
HID = 288
LANES = 256

NC = 2
SL = SLOTS // NC
RC = N * SL

FULL, TOP, BOTTOM = range(3)

ORDER = (
    ("o1", "o2"),
    ("d0", "c10", "u0", "c20", "c00", "c02", "c01", "o3"),
    ("d1", "u1", "u2", "d2", "c30"),
    ("c11", "c22", "l0", "c21"),
    ("d3", "u3", "c12", "c03"),
    ("c32", "l1", "c31"),
    ("l2", "c13", "l3"),
    ("c23", "c33"),
)

score_scale = 192.0 ** (-0.5)


def kernel(
    len_ref, bt_ref, q_hbm, pool_hbm, res_hbm, gain_hbm, uv_hbm, ow_hbm, gw_hbm, uw_hbm,
    mixed_ref, activ_ref,
    q_v, pool_v, res_v, uv_v, ow_v, gw_v, uw_v,
    gain_v, gain_w, mask_v, ctx, sbuf, cbuf, rs, rr, vbuf, mbuf, wp, acc, hid, ssq, picked, own_rows, order, out,
    load_sem, own_sem, res_send, res_recv, a2a_send, a2a_recv, ag_send, a_recv, b_recv, s_recv,
):
    me = lax.axis_index("rank")
    core = me % 2
    xx = (me // 2) % 4
    yy = me // 8
    sa = (1 - core) * 2 + core * 8
    sb = (1 - core) * 8 + core * 2
    a = (1 - core) * xx + core * yy
    b = (1 - core) * yy + core * xx
    sibling = me + 1 - 2 * core

    def rank_at(pa, pb):
        return pa * sa + pb * sb + core

    up_a, down_a = rank_at((a + 1) % 4, b), rank_at((a + 3) % 4, b)
    up_b, down_b = rank_at(a, (b + 1) % 4), rank_at(a, (b + 3) % 4)

    barrier = pltpu.get_barrier_semaphore()

    def greet(k, carry):
        pl.semaphore_signal(barrier, inc=1, device_id={"rank": (me + k) % N}, device_id_type=MESH)
        return carry

    lax.fori_loop(1, N, greet, 0)

    loads = [
        pltpu.make_async_copy(src, dst, load_sem.at[i])
        for i, (src, dst) in enumerate(
            [
                (q_hbm, q_v),
                (pool_hbm, pool_v),
                (res_hbm, res_v),
                (uv_hbm, uv_v),
                (ow_hbm, ow_v),
                (gw_hbm, gw_v),
                (uw_hbm, uw_v),
                (gain_hbm, gain_v),
            ]
        )
    ]
    for load in loads:
        load.start()

    lane = lax.broadcasted_iota(jnp.int32, (1, TOK), 1)
    page_of = lane // PAGE
    offset = lane % PAGE
    for slot in range(SLOTS):
        n = len_ref[slot]
        valid = jnp.zeros((1, TOK), F32)
        for m in range(MAXP):
            hit = (page_of == bt_ref[m, slot]) & (offset + m * PAGE < n)
            valid = jnp.where(hit, 1.0, valid)
        mask_v[slot // 4, slot % 4 : slot % 4 + 1, :] = valid
    acc[...] = jnp.zeros_like(acc)
    hid[...] = jnp.zeros_like(hid)
    ssq[...] = jnp.zeros_like(ssq)
    row = lax.broadcasted_iota(jnp.int32, (NC * RC, NC * RC), 0)
    col = lax.broadcasted_iota(jnp.int32, (NC * RC, NC * RC), 1)
    home = (row % RC) // SL * SLOTS + row // RC * SL + row % SL
    order[...] = jnp.where(home == col, 1.0, 0.0).astype(BF16)
    for ch in range(NC):
        slot = lax.broadcasted_iota(jnp.int32, (SLOTS, RC), 0)
        col = lax.broadcasted_iota(jnp.int32, (SLOTS, RC), 1)
        hit = (slot // SL == ch) & (col == me * SL + slot % SL)
        own_rows[ch] = jnp.where(hit, 1.0, 0.0).astype(BF16)

    loads[0].wait()
    loads[1].wait()

    def dest_of(k):
        p = (k * 11) % N
        return ((yy + p // 8) % 4) * 8 + ((xx + (p // 2) % 4) % 4) * 2 + (core + p % 2) % 2

    def attend(first, carry):
        q = q_v[pl.ds(first * 4, 4)].reshape(4 * HEADS, WIDTH)
        scores = lax.dot_general(
            q, pool_v[...].reshape(TOK, WIDTH), (((1,), (1,)), ((), ())), preferred_element_type=F32
        ) * score_scale
        ok = jnp.broadcast_to(
            mask_v[first][:, None, :], (4, HEADS, TOK)
        ).reshape(4 * HEADS, TOK) > 0.0
        scores = jnp.where(ok, scores, -1e30)
        peak = jnp.max(scores, axis=1, keepdims=True)
        expo = jnp.where(ok, jnp.exp(scores - peak), 0.0)
        total = jnp.sum(expo, axis=1, keepdims=True)
        total = jnp.where(total > 0.0, total, 1.0)
        weights = (expo / total).astype(BF16)
        out = jnp.dot(weights, pool_v[...].reshape(TOK, WIDTH)[:, :LAT], preferred_element_type=F32)
        for part in range(LAT // 128):
            ctx[part, pl.ds(pl.multiple_of(first * 4 * HEADS, 4 * HEADS), 4 * HEADS), :] = out[
                :, part * 128 : (part + 1) * 128
            ]
        return carry

    own_ctx = []
    for ch in range(NC):
        lax.fori_loop(ch * SL // 4, (ch + 1) * SL // 4, attend, 0)

        def pack(r, carry, ch=ch):
            for part in range(LAT // 128):
                pair = [
                    ctx[part, pl.ds(ch * SL * HEADS + 2 * r + h, SL, stride=HEADS), :] for h in range(2)
                ]
                sbuf[ch, r, :, part * 128 : (part + 1) * 128] = jnp.concatenate(pair, axis=0).astype(BF16)
            return carry

        lax.fori_loop(0, N, pack, 0)

        if ch == 0:
            pl.semaphore_wait(barrier, N - 1)

        def send_ctx(k, carry, ch=ch):
            to = dest_of(k)
            pltpu.make_async_remote_copy(
                src_ref=sbuf.at[ch, to], dst_ref=cbuf.at[ch, me],
                send_sem=a2a_send.at[ch], recv_sem=a2a_recv.at[ch],
                device_id={"rank": to}, device_id_type=MESH,
            ).start()
            return carry

        lax.fori_loop(1, N, send_ctx, 0)
        own_ctx.append(pltpu.make_async_copy(sbuf.at[ch, me], cbuf.at[ch, me], own_sem.at[ch]))
        own_ctx[ch].start()

    loads[2].wait()
    for r in range(N):
        rs[r, :, 0:COLS] = res_v[:, r * COLS : (r + 1) * COLS]
        rs[r, :, COLS:LANES] = jnp.zeros((SLOTS, LANES - COLS), BF16)

    def send_res(k, carry):
        to = dest_of(k)
        pltpu.make_async_remote_copy(
            src_ref=rs.at[to], dst_ref=rr.at[me], send_sem=res_send, recv_sem=res_recv,
            device_id={"rank": to}, device_id_type=MESH,
        ).start()
        return carry

    lax.fori_loop(1, N, send_res, 0)
    own_res = pltpu.make_async_copy(rs.at[me], rr.at[me], own_sem.at[NC])
    own_res.start()

    for load in loads[3:]:
        load.wait()

    gain_w[...] = gain_v[...].astype(F32)

    def align(q, carry):
        lanes = pl.ds(pl.multiple_of(q * 4 * COLS, 128), 4 * COLS)
        gain = jnp.concatenate([gain_w[pl.ds(q * 7 + i, 1), :] for i in range(7)], axis=1)
        for first, w in ((0, gw_v), (HID, uw_v)):
            scaled = (w[:, lanes].astype(F32) * gain).astype(BF16)
            for i in range(4):
                wp[q * 4 + i, first : first + HID, :] = scaled[:, i * COLS : (i + 1) * COLS]
        return carry

    lax.fori_loop(0, N // 4, align, 0)

    def turn(j):
        return (4 - j + (j // 2) * 3 + (j // 3) * 2) % 4

    def shard(j, i):
        return rank_at((a + turn(j)) % 4, (b + turn(i)) % 4)

    def other_shard(j, i):
        return ((b + turn(j)) % 4) * sb + ((a + turn(i)) % 4) * sa + (1 - core)

    bufs = (vbuf, mbuf)

    def piece(g, ch, s, part):
        buf = bufs[g]
        half = buf.shape[2] // 2
        if part == FULL:
            return buf.at[ch, s]
        return buf.at[ch, s, pl.ds(0 if part == TOP else half, half)]

    def push(g, ch, ref, sem, to):
        pltpu.make_async_remote_copy(
            src_ref=ref, dst_ref=ref, send_sem=ag_send.at[g, ch], recv_sem=sem,
            device_id={"rank": to}, device_id_type=MESH,
        ).start()

    def arrive(g, ch, ref, sem):
        pltpu.make_async_remote_copy(
            src_ref=ref, dst_ref=ref, send_sem=ag_send.at[g, ch], recv_sem=sem,
            device_id={"rank": sibling}, device_id_type=MESH,
        ).wait_recv()

    def share(g, ch, j, i):
        push(g, ch, piece(g, ch, shard(j, i), FULL), s_recv.at[g, ch, j * 4 + i], sibling)

    def along_b(g, ch, j):
        full = piece(g, ch, shard(j, 0), FULL)
        push(g, ch, full, b_recv.at[g, ch, j * 4], up_b)
        push(g, ch, full, b_recv.at[g, ch, j * 4 + 1], down_b)
        share(g, ch, j, 0)

    def open_line(g, ch):
        own = piece(g, ch, me, FULL)
        push(g, ch, own, a_recv.at[g, ch, 0], up_a)
        push(g, ch, own, a_recv.at[g, ch, 1], down_a)
        along_b(g, ch, 0)

    def own_line(g, ch, j):
        s = shard(j, 0)
        if j == 1:
            arrive(g, ch, piece(g, ch, s, FULL), a_recv.at[g, ch, 0])
            push(g, ch, piece(g, ch, s, TOP), a_recv.at[g, ch, 2], up_a)
        elif j == 2:
            arrive(g, ch, piece(g, ch, s, FULL), a_recv.at[g, ch, 1])
            push(g, ch, piece(g, ch, s, BOTTOM), a_recv.at[g, ch, 3], down_a)
        else:
            arrive(g, ch, piece(g, ch, s, TOP), a_recv.at[g, ch, 2])
            arrive(g, ch, piece(g, ch, s, BOTTOM), a_recv.at[g, ch, 3])
        along_b(g, ch, j)

    def line_below(g, ch, j):
        s = shard(j, 1)
        arrive(g, ch, piece(g, ch, s, FULL), b_recv.at[g, ch, j * 4])
        push(g, ch, piece(g, ch, s, TOP), b_recv.at[g, ch, j * 4 + 2], up_b)
        share(g, ch, j, 1)

    def line_above(g, ch, j):
        s = shard(j, 2)
        arrive(g, ch, piece(g, ch, s, FULL), b_recv.at[g, ch, j * 4 + 1])
        push(g, ch, piece(g, ch, s, BOTTOM), b_recv.at[g, ch, j * 4 + 3], down_b)
        share(g, ch, j, 2)

    def last_line(g, ch, j):
        s = shard(j, 3)
        arrive(g, ch, piece(g, ch, s, TOP), b_recv.at[g, ch, j * 4 + 2])
        arrive(g, ch, piece(g, ch, s, BOTTOM), b_recv.at[g, ch, j * 4 + 3])
        share(g, ch, j, 3)

    def out_part(ch, s):
        w = ow_v[:, pl.ds(pl.multiple_of(s * LANES, LANES), LANES)]
        return lax.dot_general(w, vbuf[ch, s], (((1,), (1,)), ((), ())), preferred_element_type=F32)

    def hidden_part(ch, s):
        x = mbuf[ch, s]
        wide = x.astype(F32)
        ssq[ch] += jnp.sum((wide * wide).reshape(COLS // 8, 8, RC), axis=0)
        picked[ch, s] = lax.dot_general(own_rows[ch], x, (((1,), (1,)), ((), ())), preferred_element_type=F32)
        return jnp.dot(wp[s], x, preferred_element_type=F32)

    def compute(g, ch, j, i):
        total, part = ((acc, out_part), (hid, hidden_part))[g]
        arrive(g, ch, piece(g, ch, other_shard(j, i), FULL), s_recv.at[g, ch, j * 4 + i])
        total[ch] += part(ch, shard(j, i)) + part(ch, other_shard(j, i))

    acts = {"o": own_line, "d": line_below, "u": line_above, "l": last_line}

    def stage(g, ch, work):
        for name in work:
            if name[0] == "c":
                compute(g, ch, int(name[1]), int(name[2]))
            else:
                acts[name[0]](g, ch, int(name[1]))

    def gather(g, early, finish):
        for n, work in enumerate(ORDER):
            def body(ch, carry, work=work):
                stage(g, ch, work)
                return carry

            if n < len(ORDER) - 1:
                lax.fori_loop(0, NC, body, 0)
            else:
                for ch in range(NC):
                    stage(g, ch, work)
                    finish(ch)
            if n == 0:
                early()

    for ch in range(NC):
        own_ctx[ch].wait()
        pltpu.make_async_remote_copy(
            src_ref=sbuf.at[ch, pl.ds(0, N - 1)], dst_ref=cbuf.at[ch, pl.ds(0, N - 1)],
            send_sem=a2a_send.at[ch], recv_sem=a2a_recv.at[ch],
            device_id={"rank": sibling}, device_id_type=MESH,
        ).wait_recv()
        uv = jnp.concatenate([uv_v[0], uv_v[1]], axis=1)
        z = jnp.dot(cbuf[ch].reshape(N * 2 * SL, LAT), uv, preferred_element_type=F32)
        z = z.reshape(N, 2, SL, LANES)
        first = z[:, 0, :, :128].reshape(RC, 128)
        second = z[:, 1, :, 128:].reshape(RC, 128)
        vbuf[ch, me] = jnp.concatenate([first, second], axis=1).astype(BF16)
        open_line(0, ch)

    def add_residual():
        own_res.wait()
        pltpu.make_async_remote_copy(
            src_ref=rs.at[pl.ds(0, N - 1)], dst_ref=rr.at[pl.ds(0, N - 1)], send_sem=res_send, recv_sem=res_recv,
            device_id={"rank": sibling}, device_id_type=MESH,
        ).wait()
        for ch in range(NC):
            res = rr[...].astype(F32)[:, ch * SL : (ch + 1) * SL, :].reshape(RC, LANES)
            acc[ch] += res.T[:COLS]

    def mix(ch):
        mbuf[ch, me] = acc[ch].astype(BF16)
        open_line(1, ch)

    def finish(ch):
        factor = lax.rsqrt(jnp.sum(ssq[ch], axis=0, keepdims=True) * (1.0 / D) + 1e-6)
        gate = hid[ch, :HID] * factor
        upper = hid[ch, HID:] * factor
        activ = (gate / (1.0 + jnp.exp(-gate)) * upper).astype(BF16)
        out[ch] = jnp.dot(activ, order[ch * RC : (ch + 1) * RC, :], preferred_element_type=F32)

    gather(0, add_residual, mix)
    gather(1, lambda: None, finish)

    for s in range(N):
        rows = picked[0, s]
        for ch in range(1, NC):
            rows += picked[ch, s]
        mixed_ref[:, s * COLS : (s + 1) * COLS] = rows.astype(BF16)

    activ_ref[...] = (out[0] + out[1]).astype(BF16)

    def sent(buf, sem):
        pltpu.make_async_remote_copy(
            src_ref=buf.at[pl.ds(0, N - 1)], dst_ref=buf.at[pl.ds(0, N - 1)], send_sem=sem, recv_sem=res_recv,
            device_id={"rank": sibling}, device_id_type=MESH,
        ).wait_send()

    for ch in range(NC):
        sent(sbuf.at[ch], a2a_send.at[ch])
        sent(vbuf.at[ch], ag_send.at[0, ch])
        sent(mbuf.at[ch], ag_send.at[1, ch])


def hand_out(mixed_in, activ_in, mixed_out, activ_out, sem):
    copies = [
        pltpu.make_async_copy(mixed_in, mixed_out, sem.at[0]),
        pltpu.make_async_copy(activ_in, activ_out, sem.at[1]),
    ]
    for copy in copies:
        copy.start()
    for copy in copies:
        copy.wait()


def per_device(
    queries, cache_pool, lengths, block_table, residual, norm_gain, uv_weight, out_weight, gate_weight, up_weight
):
    gain = norm_gain.reshape(D // 128, 128)
    vmem = pl.BlockSpec(memory_space=pltpu.VMEM)
    smem = pl.BlockSpec(memory_space=pltpu.SMEM)
    hbm = pl.BlockSpec(memory_space=pl.ANY)
    dma = pltpu.SemaphoreType.DMA
    mixed, activ = pl.pallas_call(
        kernel,
        out_shape=(pltpu.VMEM((SLOTS, D), BF16), pltpu.VMEM((HID, N * SLOTS), BF16)),
        in_specs=[smem, smem] + [hbm] * 8,
        out_specs=(vmem, vmem),
        scratch_shapes=[
            pltpu.VMEM((SLOTS, HEADS, WIDTH), BF16),
            pltpu.VMEM((SLOTS, PAGE, WIDTH), BF16),
            pltpu.VMEM((SLOTS, D), BF16),
            pltpu.VMEM((2, LAT, 128), BF16),
            pltpu.VMEM((COLS, N * LANES), BF16),
            pltpu.VMEM((HID, D), BF16),
            pltpu.VMEM((HID, D), BF16),
            pltpu.VMEM((D // 128, 128), BF16),
            pltpu.VMEM((D // 128, 128), F32),
            pltpu.VMEM((SLOTS // 4, 4, TOK), F32),
            pltpu.VMEM((LAT // 128, SLOTS * HEADS, 128), F32),
            pltpu.VMEM((NC, N, 2 * SL, LAT), BF16),
            pltpu.VMEM((NC, N, 2 * SL, LAT), BF16),
            pltpu.VMEM((N, SLOTS, LANES), BF16),
            pltpu.VMEM((N, SLOTS, LANES), BF16),
            pltpu.VMEM((NC, N, RC, LANES), BF16),
            pltpu.VMEM((NC, N, COLS, RC), BF16),
            pltpu.VMEM((N, 2 * HID, COLS), BF16),
            pltpu.VMEM((NC, COLS, RC), F32),
            pltpu.VMEM((NC, 2 * HID, RC), F32),
            pltpu.VMEM((NC, 8, RC), F32),
            pltpu.VMEM((NC, N, SLOTS, COLS), F32),
            pltpu.VMEM((NC, SLOTS, RC), BF16),
            pltpu.VMEM((NC * RC, NC * RC), BF16),
            pltpu.VMEM((NC, HID, NC * RC), F32),
            dma((8,)),
            dma((NC + 1,)),
            dma,
            dma,
            dma((NC,)),
            dma((NC,)),
            dma((2, NC)),
            dma((2, NC, 4)),
            dma((2, NC, 16)),
            dma((2, NC, 16)),
        ],
        compiler_params=pltpu.CompilerParams(
            collective_id=0, has_side_effects=True, vmem_limit_bytes=60 * 1024 * 1024
        ),
        cost_estimate=pl.CostEstimate(flops=7 * 10**9, bytes_accessed=15 * 10**6, transcendentals=10**6),
    )(
        lengths, block_table.T, queries, cache_pool, residual, gain, uv_weight,
        out_weight.T, gate_weight.T, up_weight.T,
    )
    mixed, activ = pl.pallas_call(
        hand_out,
        out_shape=(
            jax.ShapeDtypeStruct((SLOTS, D), BF16),
            jax.ShapeDtypeStruct((HID, N * SLOTS), BF16),
        ),
        in_specs=[vmem, vmem],
        out_specs=(hbm, hbm),
        scratch_shapes=[dma((2,))],
    )(pltpu.with_memory_space_constraint(mixed, pltpu.VMEM), pltpu.with_memory_space_constraint(activ, pltpu.VMEM))
    return mixed, activ.T


def solution(mesh):
    placed = (
        P(("group", "rank"), None, None),
        P(("group", "rank"), None, None),
        P(("group", "rank")),
        P(("group", "rank"), None),
        P(("group", "rank"), None),
        P(),
        P("rank", None, None),
        P(None, "rank"),
        P(None, "rank"),
        P(None, "rank"),
    )
    return jax.shard_map(
        per_device,
        mesh=mesh,
        in_specs=placed,
        out_specs=(P(("group", "rank"), None), P("group", "rank")),
        check_vma=False,
    )
```

```python
import jax
import jax.numpy as jnp
from jax import lax
from jax.experimental import pallas as pl
from jax.experimental.pallas import tpu as pltpu
from jax.sharding import PartitionSpec as P

F32 = jnp.float32
BF16 = jnp.bfloat16
MESH = pl.DeviceIdType.MESH

N = 32
SLOTS = 16
HEADS = 64
LAT = 512
WIDTH = 576
TOK = 512
PAGE = 32
MAXP = 4
D = 7168
COLS = 224
HID = 288
LANES = 256

NC = 2
SL = SLOTS // NC
RC = N * SL

FULL, TOP, BOTTOM = range(3)

ORDER = (
    "o2a", "c00b", "u0a", "c00a", "o1a", "d0a", "o2b", "o1b",
    "c10a", "d0b", "c20a", "c20b", "c01a", "o3a", "d2a", "c02a",
    "c01b", "u0b", "u2a", "c10b", "d1a", "c30a", "l0a", "c21a",
    "c02b", "o3b", "u2b", "d2b", "c22a", "c11a", "c03a", "c22b",
    "u1a", "c21b", "u3a", "c30b", "d3a", "u1b", "c12a", "l2a",
    "c32a", "d1b", "c31a", "l0b", "u3b", "c23a", "d3b", "c12b",
    "l1a", "l2b", "c03b", "l3a", "c11b", "c32b", "l1b", "c13a",
    "c33a", "l3b", "c13b", "c23b", "c31b", "c33b",
)

score_scale = 192.0 ** (-0.5)


def kernel(
    len_ref, bt_ref, q_hbm, pool_hbm, res_hbm, gain_hbm, uv_hbm, ow_hbm, gw_hbm, uw_hbm,
    mixed_ref, activ_ref,
    q_v, pool_v, res_v, uv_v, ow_v, gw_v, uw_v,
    gain_v, gain_w, mask_v, ctx, sbuf, cbuf, rs, rr, vbuf, mbuf, wp, acc, hid, ssq, picked, own_rows, order, out,
    load_sem, own_sem, res_send, res_recv, a2a_send, a2a_recv, ag_send, a_recv, b_recv, s_recv,
):
    me = lax.axis_index("rank")
    core = me % 2
    xx = (me // 2) % 4
    yy = me // 8
    sa = (1 - core) * 2 + core * 8
    sb = (1 - core) * 8 + core * 2
    a = (1 - core) * xx + core * yy
    b = (1 - core) * yy + core * xx
    sibling = me + 1 - 2 * core

    def rank_at(pa, pb):
        return pa * sa + pb * sb + core

    up_a, down_a = rank_at((a + 1) % 4, b), rank_at((a + 3) % 4, b)
    up_b, down_b = rank_at(a, (b + 1) % 4), rank_at(a, (b + 3) % 4)

    parts = [
        (q_hbm.at[pl.ds(0, SL)], q_v.at[pl.ds(0, SL)]),
        (pool_hbm, pool_v),
        (q_hbm.at[pl.ds(SL, SL)], q_v.at[pl.ds(SL, SL)]),
        (res_hbm, res_v),
        (uv_hbm, uv_v),
        (ow_hbm, ow_v),
        (gw_hbm, gw_v),
        (uw_hbm, uw_v),
        (gain_hbm, gain_v),
    ]
    loads = [pltpu.make_async_copy(src, dst, load_sem.at[n]) for n, (src, dst) in enumerate(parts)]
    for load in loads[:2]:
        load.start()

    barrier = pltpu.get_barrier_semaphore()

    def greet(k, carry):
        pl.semaphore_signal(barrier, inc=1, device_id={"rank": (me + k) % N}, device_id_type=MESH)
        return carry

    lax.fori_loop(1, N, greet, 0)
    loads[2].start()

    lane = lax.broadcasted_iota(jnp.int32, (1, TOK), 1)
    page_of = lane // PAGE
    offset = lane % PAGE
    for slot in range(SLOTS):
        n = len_ref[slot]
        valid = jnp.zeros((1, TOK), F32)
        for m in range(MAXP):
            hit = (page_of == bt_ref[m, slot]) & (offset + m * PAGE < n)
            valid = jnp.where(hit, 1.0, valid)
        mask_v[slot // 4, slot % 4 : slot % 4 + 1, :] = valid
    loads[0].wait()
    loads[1].wait()

    def dest_of(k):
        p = (k * 11) % N
        return ((yy + p // 8) % 4) * 8 + ((xx + (p // 2) % 4) % 4) * 2 + (core + p % 2) % 2

    def attend(first, carry):
        q = q_v[pl.ds(first * 4, 4)].reshape(4 * HEADS, WIDTH)
        scores = lax.dot_general(
            q, pool_v[...].reshape(TOK, WIDTH), (((1,), (1,)), ((), ())), preferred_element_type=F32
        ) * score_scale
        ok = jnp.broadcast_to(
            mask_v[first][:, None, :], (4, HEADS, TOK)
        ).reshape(4 * HEADS, TOK) > 0.0
        scores = jnp.where(ok, scores, -1e30)
        peak = jnp.max(scores, axis=1, keepdims=True)
        expo = jnp.where(ok, jnp.exp(scores - peak), 0.0)
        total = jnp.sum(expo, axis=1, keepdims=True)
        total = jnp.where(total > 0.0, total, 1.0)
        weights = (expo / total).astype(BF16)
        out = jnp.dot(weights, pool_v[...].reshape(TOK, WIDTH)[:, :LAT], preferred_element_type=F32)
        for part in range(LAT // 128):
            ctx[part, pl.ds(pl.multiple_of(first * 4 * HEADS, 4 * HEADS), 4 * HEADS), :] = out[
                :, part * 128 : (part + 1) * 128
            ]
        return carry

    own_ctx = []
    for ch in range(NC):
        if ch == 1:
            loads[2].wait()
        lax.fori_loop(ch * SL // 4, (ch + 1) * SL // 4, attend, 0)

        def pack(r, carry, ch=ch):
            for part in range(LAT // 128):
                pair = [
                    ctx[part, pl.ds(ch * SL * HEADS + 2 * r + h, SL, stride=HEADS), :] for h in range(2)
                ]
                sbuf[ch, r, :, part * 128 : (part + 1) * 128] = jnp.concatenate(pair, axis=0).astype(BF16)
            return carry

        lax.fori_loop(0, N, pack, 0)

        if ch == 0:
            pl.semaphore_wait(barrier, N - 1)

        def send_ctx(k, carry, ch=ch):
            to = dest_of(k)
            pltpu.make_async_remote_copy(
                src_ref=sbuf.at[ch, to], dst_ref=cbuf.at[ch, me],
                send_sem=a2a_send.at[ch], recv_sem=a2a_recv.at[ch],
                device_id={"rank": to}, device_id_type=MESH,
            ).start()
            return carry

        lax.fori_loop(1, N, send_ctx, 0)
        own_ctx.append(pltpu.make_async_copy(sbuf.at[ch, me], cbuf.at[ch, me], own_sem.at[ch]))
        own_ctx[ch].start()
        if ch == 0:
            for load in loads[3:]:
                load.start()

    loads[3].wait()
    for r in range(N):
        rs[r, :, 0:COLS] = res_v[:, r * COLS : (r + 1) * COLS]
        rs[r, :, COLS:LANES] = jnp.zeros((SLOTS, LANES - COLS), BF16)

    def send_res(k, carry):
        to = dest_of(k)
        pltpu.make_async_remote_copy(
            src_ref=rs.at[to], dst_ref=rr.at[me], send_sem=res_send, recv_sem=res_recv,
            device_id={"rank": to}, device_id_type=MESH,
        ).start()
        return carry

    lax.fori_loop(1, N, send_res, 0)
    own_res = pltpu.make_async_copy(rs.at[me], rr.at[me], own_sem.at[NC])
    own_res.start()

    acc[...] = jnp.zeros_like(acc)
    hid[...] = jnp.zeros_like(hid)
    ssq[...] = jnp.zeros_like(ssq)
    row = lax.broadcasted_iota(jnp.int32, (NC * RC, NC * RC), 0)
    col = lax.broadcasted_iota(jnp.int32, (NC * RC, NC * RC), 1)
    home = (row % RC) // SL * SLOTS + row // RC * SL + row % SL
    order[...] = jnp.where(home == col, 1.0, 0.0).astype(BF16)
    for ch in range(NC):
        slot = lax.broadcasted_iota(jnp.int32, (SLOTS, RC), 0)
        col = lax.broadcasted_iota(jnp.int32, (SLOTS, RC), 1)
        hit = (slot // SL == ch) & (col == me * SL + slot % SL)
        own_rows[ch] = jnp.where(hit, 1.0, 0.0).astype(BF16)

    for load in loads[4:]:
        load.wait()

    gain_w[...] = gain_v[...].astype(F32)

    def align(q, carry):
        lanes = pl.ds(pl.multiple_of(q * 4 * COLS, 128), 4 * COLS)
        gain = jnp.concatenate([gain_w[pl.ds(q * 7 + i, 1), :] for i in range(7)], axis=1)
        for first, w in ((0, gw_v), (HID, uw_v)):
            scaled = (w[:, lanes].astype(F32) * gain).astype(BF16)
            for i in range(4):
                wp[q * 4 + i, first : first + HID, :] = scaled[:, i * COLS : (i + 1) * COLS]
        return carry

    lax.fori_loop(0, N // 4, align, 0)

    def turn(j):
        return (4 - j + (j // 2) * 3 + (j // 3) * 2) % 4

    def shard(j, i):
        return rank_at((a + turn(j)) % 4, (b + turn(i)) % 4)

    def other_shard(j, i):
        return ((b + turn(j)) % 4) * sb + ((a + turn(i)) % 4) * sa + (1 - core)

    bufs = (vbuf, mbuf)

    def piece(g, ch, s, part):
        buf = bufs[g]
        half = buf.shape[2] // 2
        if part == FULL:
            return buf.at[ch, s]
        return buf.at[ch, s, pl.ds(0 if part == TOP else half, half)]

    def push(g, ch, ref, sem, to):
        pltpu.make_async_remote_copy(
            src_ref=ref, dst_ref=ref, send_sem=ag_send.at[g, ch], recv_sem=sem,
            device_id={"rank": to}, device_id_type=MESH,
        ).start()

    def arrive(g, ch, ref, sem):
        pltpu.make_async_remote_copy(
            src_ref=ref, dst_ref=ref, send_sem=ag_send.at[g, ch], recv_sem=sem,
            device_id={"rank": sibling}, device_id_type=MESH,
        ).wait_recv()

    def share(g, ch, j, i):
        push(g, ch, piece(g, ch, shard(j, i), FULL), s_recv.at[g, ch, j * 4 + i], sibling)

    def along_b(g, ch, j):
        full = piece(g, ch, shard(j, 0), FULL)
        push(g, ch, full, b_recv.at[g, ch, j * 4], up_b)
        push(g, ch, full, b_recv.at[g, ch, j * 4 + 1], down_b)
        share(g, ch, j, 0)

    def open_line(g, ch):
        own = piece(g, ch, me, FULL)
        push(g, ch, own, a_recv.at[g, ch, 0], up_a)
        push(g, ch, own, a_recv.at[g, ch, 1], down_a)
        along_b(g, ch, 0)

    def own_line(g, ch, j):
        s = shard(j, 0)
        if j == 1:
            arrive(g, ch, piece(g, ch, s, FULL), a_recv.at[g, ch, 0])
            push(g, ch, piece(g, ch, s, TOP), a_recv.at[g, ch, 2], up_a)
        elif j == 2:
            arrive(g, ch, piece(g, ch, s, FULL), a_recv.at[g, ch, 1])
            push(g, ch, piece(g, ch, s, BOTTOM), a_recv.at[g, ch, 3], down_a)
        else:
            arrive(g, ch, piece(g, ch, s, TOP), a_recv.at[g, ch, 2])
            arrive(g, ch, piece(g, ch, s, BOTTOM), a_recv.at[g, ch, 3])
        along_b(g, ch, j)

    def line_below(g, ch, j):
        s = shard(j, 1)
        arrive(g, ch, piece(g, ch, s, FULL), b_recv.at[g, ch, j * 4])
        push(g, ch, piece(g, ch, s, TOP), b_recv.at[g, ch, j * 4 + 2], up_b)
        share(g, ch, j, 1)

    def line_above(g, ch, j):
        s = shard(j, 2)
        arrive(g, ch, piece(g, ch, s, FULL), b_recv.at[g, ch, j * 4 + 1])
        push(g, ch, piece(g, ch, s, BOTTOM), b_recv.at[g, ch, j * 4 + 3], down_b)
        share(g, ch, j, 2)

    def last_line(g, ch, j):
        s = shard(j, 3)
        arrive(g, ch, piece(g, ch, s, TOP), b_recv.at[g, ch, j * 4 + 2])
        arrive(g, ch, piece(g, ch, s, BOTTOM), b_recv.at[g, ch, j * 4 + 3])
        share(g, ch, j, 3)

    def out_part(ch, s):
        w = ow_v[:, pl.ds(pl.multiple_of(s * LANES, LANES), LANES)]
        return lax.dot_general(w, vbuf[ch, s], (((1,), (1,)), ((), ())), preferred_element_type=F32)

    def hidden_part(ch, s):
        x = mbuf[ch, s]
        wide = x.astype(F32)
        ssq[ch] += jnp.sum((wide * wide).reshape(COLS // 8, 8, RC), axis=0)
        picked[ch, s] = lax.dot_general(own_rows[ch], x, (((1,), (1,)), ((), ())), preferred_element_type=F32)
        return jnp.dot(wp[s], x, preferred_element_type=F32)

    def compute(g, ch, j, i):
        total, part = ((acc, out_part), (hid, hidden_part))[g]
        arrive(g, ch, piece(g, ch, other_shard(j, i), FULL), s_recv.at[g, ch, j * 4 + i])
        total[ch] += part(ch, shard(j, i)) + part(ch, other_shard(j, i))

    acts = {"o": own_line, "d": line_below, "u": line_above, "l": last_line}

    def gather(g, early, finish):
        left = [len(ORDER) // NC] * NC
        for n, name in enumerate(ORDER):
            ch = "ab".index(name[-1])
            if name[0] == "c":
                compute(g, ch, int(name[1]), int(name[2]))
            else:
                acts[name[0]](g, ch, int(name[1]))
            left[ch] -= 1
            if left[ch] == 0:
                finish(ch)
            if n == 6:
                early()

    for ch in range(NC):
        own_ctx[ch].wait()
        pltpu.make_async_remote_copy(
            src_ref=sbuf.at[ch, pl.ds(0, N - 1)], dst_ref=cbuf.at[ch, pl.ds(0, N - 1)],
            send_sem=a2a_send.at[ch], recv_sem=a2a_recv.at[ch],
            device_id={"rank": sibling}, device_id_type=MESH,
        ).wait_recv()
        uv = jnp.concatenate([uv_v[0], uv_v[1]], axis=1)
        z = jnp.dot(cbuf[ch].reshape(N * 2 * SL, LAT), uv, preferred_element_type=F32)
        z = z.reshape(N, 2, SL, LANES)
        first = z[:, 0, :, :128].reshape(RC, 128)
        second = z[:, 1, :, 128:].reshape(RC, 128)
        vbuf[ch, me] = jnp.concatenate([first, second], axis=1).astype(BF16)
        open_line(0, ch)

    def add_residual():
        own_res.wait()
        pltpu.make_async_remote_copy(
            src_ref=rs.at[pl.ds(0, N - 1)], dst_ref=rr.at[pl.ds(0, N - 1)], send_sem=res_send, recv_sem=res_recv,
            device_id={"rank": sibling}, device_id_type=MESH,
        ).wait()
        for ch in range(NC):
            res = rr[...].astype(F32)[:, ch * SL : (ch + 1) * SL, :].reshape(RC, LANES)
            acc[ch] += res.T[:COLS]

    def mix(ch):
        mbuf[ch, me] = acc[ch].astype(BF16)
        open_line(1, ch)

    def finish(ch):
        factor = lax.rsqrt(jnp.sum(ssq[ch], axis=0, keepdims=True) * (1.0 / D) + 1e-6)
        gate = hid[ch, :HID] * factor
        upper = hid[ch, HID:] * factor
        activ = (gate / (1.0 + jnp.exp(-gate)) * upper).astype(BF16)
        out[ch] = jnp.dot(activ, order[ch * RC : (ch + 1) * RC, :], preferred_element_type=F32)

    gather(0, add_residual, mix)
    gather(1, lambda: None, finish)

    for s in range(N):
        rows = picked[0, s]
        for ch in range(1, NC):
            rows += picked[ch, s]
        mixed_ref[:, s * COLS : (s + 1) * COLS] = rows.astype(BF16)

    activ_ref[...] = (out[0] + out[1]).astype(BF16)

    def sent(buf, sem):
        pltpu.make_async_remote_copy(
            src_ref=buf.at[pl.ds(0, N - 1)], dst_ref=buf.at[pl.ds(0, N - 1)], send_sem=sem, recv_sem=res_recv,
            device_id={"rank": sibling}, device_id_type=MESH,
        ).wait_send()

    for ch in range(NC):
        sent(sbuf.at[ch], a2a_send.at[ch])
        sent(vbuf.at[ch], ag_send.at[0, ch])
        sent(mbuf.at[ch], ag_send.at[1, ch])


def hand_out(mixed_in, activ_in, mixed_out, activ_out, sem):
    copies = [
        pltpu.make_async_copy(mixed_in, mixed_out, sem.at[0]),
        pltpu.make_async_copy(activ_in, activ_out, sem.at[1]),
    ]
    for copy in copies:
        copy.start()
    for copy in copies:
        copy.wait()


def per_device(
    queries, cache_pool, lengths, block_table, residual, norm_gain, uv_weight, out_weight, gate_weight, up_weight
):
    gain = norm_gain.reshape(D // 128, 128)
    vmem = pl.BlockSpec(memory_space=pltpu.VMEM)
    smem = pl.BlockSpec(memory_space=pltpu.SMEM)
    hbm = pl.BlockSpec(memory_space=pl.ANY)
    dma = pltpu.SemaphoreType.DMA
    mixed, activ = pl.pallas_call(
        kernel,
        out_shape=(pltpu.VMEM((SLOTS, D), BF16), pltpu.VMEM((HID, N * SLOTS), BF16)),
        in_specs=[smem, smem] + [hbm] * 8,
        out_specs=(vmem, vmem),
        scratch_shapes=[
            pltpu.VMEM((SLOTS, HEADS, WIDTH), BF16),
            pltpu.VMEM((SLOTS, PAGE, WIDTH), BF16),
            pltpu.VMEM((SLOTS, D), BF16),
            pltpu.VMEM((2, LAT, 128), BF16),
            pltpu.VMEM((COLS, N * LANES), BF16),
            pltpu.VMEM((HID, D), BF16),
            pltpu.VMEM((HID, D), BF16),
            pltpu.VMEM((D // 128, 128), BF16),
            pltpu.VMEM((D // 128, 128), F32),
            pltpu.VMEM((SLOTS // 4, 4, TOK), F32),
            pltpu.VMEM((LAT // 128, SLOTS * HEADS, 128), F32),
            pltpu.VMEM((NC, N, 2 * SL, LAT), BF16),
            pltpu.VMEM((NC, N, 2 * SL, LAT), BF16),
            pltpu.VMEM((N, SLOTS, LANES), BF16),
            pltpu.VMEM((N, SLOTS, LANES), BF16),
            pltpu.VMEM((NC, N, RC, LANES), BF16),
            pltpu.VMEM((NC, N, COLS, RC), BF16),
            pltpu.VMEM((N, 2 * HID, COLS), BF16),
            pltpu.VMEM((NC, COLS, RC), F32),
            pltpu.VMEM((NC, 2 * HID, RC), F32),
            pltpu.VMEM((NC, 8, RC), F32),
            pltpu.VMEM((NC, N, SLOTS, COLS), F32),
            pltpu.VMEM((NC, SLOTS, RC), BF16),
            pltpu.VMEM((NC * RC, NC * RC), BF16),
            pltpu.VMEM((NC, HID, NC * RC), F32),
            dma((9,)),
            dma((NC + 1,)),
            dma,
            dma,
            dma((NC,)),
            dma((NC,)),
            dma((2, NC)),
            dma((2, NC, 4)),
            dma((2, NC, 16)),
            dma((2, NC, 16)),
        ],
        compiler_params=pltpu.CompilerParams(
            collective_id=0, has_side_effects=True, vmem_limit_bytes=60 * 1024 * 1024
        ),
        cost_estimate=pl.CostEstimate(flops=7 * 10**9, bytes_accessed=15 * 10**6, transcendentals=10**6),
    )(
        lengths, block_table.T, queries, cache_pool, residual, gain, uv_weight,
        out_weight.T, gate_weight.T, up_weight.T,
    )
    mixed, activ = pl.pallas_call(
        hand_out,
        out_shape=(
            jax.ShapeDtypeStruct((SLOTS, D), BF16),
            jax.ShapeDtypeStruct((HID, N * SLOTS), BF16),
        ),
        in_specs=[vmem, vmem],
        out_specs=(hbm, hbm),
        scratch_shapes=[dma((2,))],
    )(pltpu.with_memory_space_constraint(mixed, pltpu.VMEM), pltpu.with_memory_space_constraint(activ, pltpu.VMEM))
    return mixed, activ.T


def solution(mesh):
    placed = (
        P(("group", "rank"), None, None),
        P(("group", "rank"), None, None),
        P(("group", "rank")),
        P(("group", "rank"), None),
        P(("group", "rank"), None),
        P(),
        P("rank", None, None),
        P(None, "rank"),
        P(None, "rank"),
        P(None, "rank"),
    )
    return jax.shard_map(
        per_device,
        mesh=mesh,
        in_specs=placed,
        out_specs=(P(("group", "rank"), None), P("group", "rank")),
        check_vma=False,
    )
```

```python
import jax
import jax.numpy as jnp
from jax import lax
from jax.experimental import pallas as pl
from jax.experimental.pallas import tpu as pltpu
from jax.sharding import PartitionSpec as P

F32 = jnp.float32
BF16 = jnp.bfloat16
MESH = pl.DeviceIdType.MESH

N = 32
SLOTS = 16
HEADS = 64
LAT = 512
WIDTH = 576
TOK = 512
PAGE = 32
MAXP = 4
D = 7168
COLS = 224
HID = 288
LANES = 256

NC = 2
SL = SLOTS // NC
RC = N * SL

FULL, TOP, BOTTOM = range(3)

FAR_FIRST = sorted(
    ((dy, dx, dc) for dy in range(4) for dx in range(4) for dc in range(2) if dy + dx + dc > 0),
    key=lambda d: -(min(d[0], 4 - d[0]) + min(d[1], 4 - d[1])),
)

ORDER = (
    "o1a", "o2a", "o1b", "o2b", "c00b", "d0a", "c10a", "c01a",
    "o3a", "c10b", "d1a", "c20b", "u1a", "d2a", "c00a", "u0a",
    "u2a", "c30a", "c11a", "c20a", "c02a", "o3b", "d1b", "c12a",
    "c22a", "u1b", "c21a", "c11b", "u3a", "u0b", "c30b", "d3a",
    "c12b", "d0b", "d2b", "l1a", "c32a", "c02b", "l2a", "c31a",
    "u2b", "c21b", "u3b", "l0a", "d3b", "c23a", "c13a", "c22b",
    "l3a", "l1b", "c32b", "c31b", "l0b", "c03a", "c33a", "l2b",
    "l3b", "c01b", "c13b", "c03b", "c23b", "c33b",
)

score_scale = 192.0 ** (-0.5)


def kernel(
    len_ref, bt_ref, q_hbm, pool_hbm, res_hbm, gain_hbm, uv_hbm, ow_hbm, gw_hbm, uw_hbm,
    mixed_ref, activ_ref,
    q_v, pool_v, res_v, uv_v, ow_v, gw_v, uw_v,
    gain_v, gain_w, mask_v, ctx, sbuf, cbuf, rs, rr, vbuf, mbuf, wp, acc, hid, ssq, picked, own_rows, order, out,
    load_sem, own_sem, res_send, res_recv, a2a_send, a2a_recv, ag_send, a_recv, b_recv, s_recv,
):
    me = lax.axis_index("rank")
    core = me % 2
    xx = (me // 2) % 4
    yy = me // 8
    sa = (1 - core) * 2 + core * 8
    sb = (1 - core) * 8 + core * 2
    a = (1 - core) * xx + core * yy
    b = (1 - core) * yy + core * xx
    sibling = me + 1 - 2 * core

    def rank_at(pa, pb):
        return pa * sa + pb * sb + core

    up_a, down_a = rank_at((a + 1) % 4, b), rank_at((a + 3) % 4, b)
    up_b, down_b = rank_at(a, (b + 1) % 4), rank_at(a, (b + 3) % 4)

    parts = [
        (q_hbm.at[pl.ds(0, SL)], q_v.at[pl.ds(0, SL)]),
        (pool_hbm, pool_v),
        (q_hbm.at[pl.ds(SL, SL)], q_v.at[pl.ds(SL, SL)]),
        (res_hbm, res_v),
        (uv_hbm, uv_v),
        (ow_hbm, ow_v),
        (gw_hbm, gw_v),
        (uw_hbm, uw_v),
        (gain_hbm, gain_v),
    ]
    loads = [pltpu.make_async_copy(src, dst, load_sem.at[n]) for n, (src, dst) in enumerate(parts)]
    for load in loads[:2]:
        load.start()

    barrier = pltpu.get_barrier_semaphore()

    def greet(k, carry):
        pl.semaphore_signal(barrier, inc=1, device_id={"rank": (me + k) % N}, device_id_type=MESH)
        return carry

    lax.fori_loop(1, N, greet, 0)
    loads[2].start()

    lane = lax.broadcasted_iota(jnp.int32, (1, TOK), 1)
    page_of = lane // PAGE
    offset = lane % PAGE
    for slot in range(SLOTS):
        n = len_ref[slot]
        valid = jnp.zeros((1, TOK), F32)
        for m in range(MAXP):
            hit = (page_of == bt_ref[m, slot]) & (offset + m * PAGE < n)
            valid = jnp.where(hit, 1.0, valid)
        mask_v[slot // 4, slot % 4 : slot % 4 + 1, :] = valid
    loads[0].wait()
    loads[1].wait()

    def dest_of(k):
        dy, dx, dc = FAR_FIRST[k]
        return ((yy + dy) % 4) * 8 + ((xx + dx) % 4) * 2 + (core + dc) % 2

    def attend(first, carry):
        q = q_v[pl.ds(first * 4, 4)].reshape(4 * HEADS, WIDTH)
        scores = lax.dot_general(
            q, pool_v[...].reshape(TOK, WIDTH), (((1,), (1,)), ((), ())), preferred_element_type=F32
        ) * score_scale
        ok = jnp.broadcast_to(
            mask_v[first][:, None, :], (4, HEADS, TOK)
        ).reshape(4 * HEADS, TOK) > 0.0
        scores = jnp.where(ok, scores, -1e30)
        peak = jnp.max(scores, axis=1, keepdims=True)
        expo = jnp.where(ok, jnp.exp(scores - peak), 0.0)
        total = jnp.sum(expo, axis=1, keepdims=True)
        total = jnp.where(total > 0.0, total, 1.0)
        weights = (expo / total).astype(BF16)
        out = jnp.dot(weights, pool_v[...].reshape(TOK, WIDTH)[:, :LAT], preferred_element_type=F32)
        for part in range(LAT // 128):
            ctx[part, pl.ds(pl.multiple_of(first * 4 * HEADS, 4 * HEADS), 4 * HEADS), :] = out[
                :, part * 128 : (part + 1) * 128
            ]
        return carry

    own_ctx = []
    for ch in range(NC):
        if ch == 1:
            loads[2].wait()
        lax.fori_loop(ch * SL // 4, (ch + 1) * SL // 4, attend, 0)

        def pack(r, carry, ch=ch):
            for part in range(LAT // 128):
                pair = [
                    ctx[part, pl.ds(ch * SL * HEADS + 2 * r + h, SL, stride=HEADS), :] for h in range(2)
                ]
                sbuf[ch, r, :, part * 128 : (part + 1) * 128] = jnp.concatenate(pair, axis=0).astype(BF16)
            return carry

        lax.fori_loop(0, N, pack, 0)

        if ch == 0:
            pl.semaphore_wait(barrier, N - 1)

        def send_ctx(k, carry, ch=ch):
            to = dest_of(k)
            pltpu.make_async_remote_copy(
                src_ref=sbuf.at[ch, to], dst_ref=cbuf.at[ch, me],
                send_sem=a2a_send.at[ch], recv_sem=a2a_recv.at[ch],
                device_id={"rank": to}, device_id_type=MESH,
            ).start()
            return carry

        for k in range(N - 1):
            send_ctx(k, 0)
        own_ctx.append(pltpu.make_async_copy(sbuf.at[ch, me], cbuf.at[ch, me], own_sem.at[ch]))
        own_ctx[ch].start()
        if ch == 0:
            for load in loads[3:]:
                load.start()

    loads[3].wait()
    for r in range(N):
        rs[r, :, 0:COLS] = res_v[:, r * COLS : (r + 1) * COLS]
        rs[r, :, COLS:LANES] = jnp.zeros((SLOTS, LANES - COLS), BF16)

    def send_res(k, carry):
        to = dest_of(k)
        pltpu.make_async_remote_copy(
            src_ref=rs.at[to], dst_ref=rr.at[me], send_sem=res_send, recv_sem=res_recv,
            device_id={"rank": to}, device_id_type=MESH,
        ).start()
        return carry

    for k in range(N - 1):
        send_res(k, 0)
    own_res = pltpu.make_async_copy(rs.at[me], rr.at[me], own_sem.at[NC])
    own_res.start()

    acc[...] = jnp.zeros_like(acc)
    hid[...] = jnp.zeros_like(hid)
    ssq[...] = jnp.zeros_like(ssq)
    row = lax.broadcasted_iota(jnp.int32, (NC * RC, NC * RC), 0)
    col = lax.broadcasted_iota(jnp.int32, (NC * RC, NC * RC), 1)
    home = (row % RC) // SL * SLOTS + row // RC * SL + row % SL
    order[...] = jnp.where(home == col, 1.0, 0.0).astype(BF16)
    for ch in range(NC):
        slot = lax.broadcasted_iota(jnp.int32, (SLOTS, RC), 0)
        col = lax.broadcasted_iota(jnp.int32, (SLOTS, RC), 1)
        hit = (slot // SL == ch) & (col == me * SL + slot % SL)
        own_rows[ch] = jnp.where(hit, 1.0, 0.0).astype(BF16)

    for load in loads[4:]:
        load.wait()

    gain_w[...] = gain_v[...].astype(F32)

    def align(q, carry):
        lanes = pl.ds(pl.multiple_of(q * 4 * COLS, 128), 4 * COLS)
        gain = jnp.concatenate([gain_w[pl.ds(q * 7 + i, 1), :] for i in range(7)], axis=1)
        for first, w in ((0, gw_v), (HID, uw_v)):
            scaled = (w[:, lanes].astype(F32) * gain).astype(BF16)
            for i in range(4):
                wp[q * 4 + i, first : first + HID, :] = scaled[:, i * COLS : (i + 1) * COLS]
        return carry

    lax.fori_loop(0, N // 4, align, 0)

    def turn(j):
        return (4 - j + (j // 2) * 3 + (j // 3) * 2) % 4

    def shard(j, i):
        return rank_at((a + turn(j)) % 4, (b + turn(i)) % 4)

    def other_shard(j, i):
        return ((b + turn(j)) % 4) * sb + ((a + turn(i)) % 4) * sa + (1 - core)

    bufs = (vbuf, mbuf)

    def piece(g, ch, s, part):
        buf = bufs[g]
        half = buf.shape[2] // 2
        if part == FULL:
            return buf.at[ch, s]
        return buf.at[ch, s, pl.ds(0 if part == TOP else half, half)]

    def push(g, ch, ref, sem, to):
        pltpu.make_async_remote_copy(
            src_ref=ref, dst_ref=ref, send_sem=ag_send.at[g, ch], recv_sem=sem,
            device_id={"rank": to}, device_id_type=MESH,
        ).start()

    def arrive(g, ch, ref, sem):
        pltpu.make_async_remote_copy(
            src_ref=ref, dst_ref=ref, send_sem=ag_send.at[g, ch], recv_sem=sem,
            device_id={"rank": sibling}, device_id_type=MESH,
        ).wait_recv()

    def share(g, ch, j, i):
        push(g, ch, piece(g, ch, shard(j, i), FULL), s_recv.at[g, ch, j * 4 + i], sibling)

    def along_b(g, ch, j):
        full = piece(g, ch, shard(j, 0), FULL)
        push(g, ch, full, b_recv.at[g, ch, j * 4], up_b)
        push(g, ch, full, b_recv.at[g, ch, j * 4 + 1], down_b)
        share(g, ch, j, 0)

    def open_line(g, ch):
        own = piece(g, ch, me, FULL)
        push(g, ch, own, a_recv.at[g, ch, 0], up_a)
        push(g, ch, own, a_recv.at[g, ch, 1], down_a)
        along_b(g, ch, 0)

    def own_line(g, ch, j):
        s = shard(j, 0)
        if j == 1:
            arrive(g, ch, piece(g, ch, s, FULL), a_recv.at[g, ch, 0])
            push(g, ch, piece(g, ch, s, TOP), a_recv.at[g, ch, 2], up_a)
        elif j == 2:
            arrive(g, ch, piece(g, ch, s, FULL), a_recv.at[g, ch, 1])
            push(g, ch, piece(g, ch, s, BOTTOM), a_recv.at[g, ch, 3], down_a)
        else:
            arrive(g, ch, piece(g, ch, s, TOP), a_recv.at[g, ch, 2])
            arrive(g, ch, piece(g, ch, s, BOTTOM), a_recv.at[g, ch, 3])
        along_b(g, ch, j)

    def line_below(g, ch, j):
        s = shard(j, 1)
        arrive(g, ch, piece(g, ch, s, FULL), b_recv.at[g, ch, j * 4])
        push(g, ch, piece(g, ch, s, TOP), b_recv.at[g, ch, j * 4 + 2], up_b)
        share(g, ch, j, 1)

    def line_above(g, ch, j):
        s = shard(j, 2)
        arrive(g, ch, piece(g, ch, s, FULL), b_recv.at[g, ch, j * 4 + 1])
        push(g, ch, piece(g, ch, s, BOTTOM), b_recv.at[g, ch, j * 4 + 3], down_b)
        share(g, ch, j, 2)

    def last_line(g, ch, j):
        s = shard(j, 3)
        arrive(g, ch, piece(g, ch, s, TOP), b_recv.at[g, ch, j * 4 + 2])
        arrive(g, ch, piece(g, ch, s, BOTTOM), b_recv.at[g, ch, j * 4 + 3])
        share(g, ch, j, 3)

    def out_part(ch, s):
        w = ow_v[:, pl.ds(pl.multiple_of(s * LANES, LANES), LANES)]
        return lax.dot_general(w, vbuf[ch, s], (((1,), (1,)), ((), ())), preferred_element_type=F32)

    def hidden_part(ch, s):
        x = mbuf[ch, s]
        wide = x.astype(F32)
        ssq[ch] += jnp.sum((wide * wide).reshape(COLS // 8, 8, RC), axis=0)
        picked[ch, s] = lax.dot_general(own_rows[ch], x, (((1,), (1,)), ((), ())), preferred_element_type=F32)
        return jnp.dot(wp[s], x, preferred_element_type=F32)

    def compute(g, ch, j, i):
        total, part = ((acc, out_part), (hid, hidden_part))[g]
        arrive(g, ch, piece(g, ch, other_shard(j, i), FULL), s_recv.at[g, ch, j * 4 + i])
        total[ch] += part(ch, shard(j, i)) + part(ch, other_shard(j, i))

    acts = {"o": own_line, "d": line_below, "u": line_above, "l": last_line}

    def gather(g, early, finish):
        left = [len(ORDER) // NC] * NC
        for n, name in enumerate(ORDER):
            ch = "ab".index(name[-1])
            if name[0] == "c":
                compute(g, ch, int(name[1]), int(name[2]))
            else:
                acts[name[0]](g, ch, int(name[1]))
            left[ch] -= 1
            if left[ch] == 0:
                finish(ch)
            if n == 6:
                early()

    for ch in range(NC):
        own_ctx[ch].wait()
        pltpu.make_async_remote_copy(
            src_ref=sbuf.at[ch, pl.ds(0, N - 1)], dst_ref=cbuf.at[ch, pl.ds(0, N - 1)],
            send_sem=a2a_send.at[ch], recv_sem=a2a_recv.at[ch],
            device_id={"rank": sibling}, device_id_type=MESH,
        ).wait_recv()
        uv = jnp.concatenate([uv_v[0], uv_v[1]], axis=1)
        z = jnp.dot(cbuf[ch].reshape(N * 2 * SL, LAT), uv, preferred_element_type=F32)
        z = z.reshape(N, 2, SL, LANES)
        first = z[:, 0, :, :128].reshape(RC, 128)
        second = z[:, 1, :, 128:].reshape(RC, 128)
        vbuf[ch, me] = jnp.concatenate([first, second], axis=1).astype(BF16)
        open_line(0, ch)

    def add_residual():
        own_res.wait()
        pltpu.make_async_remote_copy(
            src_ref=rs.at[pl.ds(0, N - 1)], dst_ref=rr.at[pl.ds(0, N - 1)], send_sem=res_send, recv_sem=res_recv,
            device_id={"rank": sibling}, device_id_type=MESH,
        ).wait()
        for ch in range(NC):
            res = rr[...].astype(F32)[:, ch * SL : (ch + 1) * SL, :].reshape(RC, LANES)
            acc[ch] += res.T[:COLS]

    def mix(ch):
        mbuf[ch, me] = acc[ch].astype(BF16)
        open_line(1, ch)

    def finish(ch):
        factor = lax.rsqrt(jnp.sum(ssq[ch], axis=0, keepdims=True) * (1.0 / D) + 1e-6)
        gate = hid[ch, :HID] * factor
        upper = hid[ch, HID:] * factor
        activ = (gate / (1.0 + jnp.exp(-gate)) * upper).astype(BF16)
        out[ch] = jnp.dot(activ, order[ch * RC : (ch + 1) * RC, :], preferred_element_type=F32)

    gather(0, add_residual, mix)
    gather(1, lambda: None, finish)

    for s in range(N):
        rows = picked[0, s]
        for ch in range(1, NC):
            rows += picked[ch, s]
        mixed_ref[:, s * COLS : (s + 1) * COLS] = rows.astype(BF16)

    activ_ref[...] = (out[0] + out[1]).astype(BF16)

    def sent(buf, sem):
        pltpu.make_async_remote_copy(
            src_ref=buf.at[pl.ds(0, N - 1)], dst_ref=buf.at[pl.ds(0, N - 1)], send_sem=sem, recv_sem=res_recv,
            device_id={"rank": sibling}, device_id_type=MESH,
        ).wait_send()

    for ch in range(NC):
        sent(sbuf.at[ch], a2a_send.at[ch])
        sent(vbuf.at[ch], ag_send.at[0, ch])
        sent(mbuf.at[ch], ag_send.at[1, ch])


def hand_out(mixed_in, activ_in, mixed_out, activ_out, sem):
    copies = [
        pltpu.make_async_copy(mixed_in, mixed_out, sem.at[0]),
        pltpu.make_async_copy(activ_in, activ_out, sem.at[1]),
    ]
    for copy in copies:
        copy.start()
    for copy in copies:
        copy.wait()


def per_device(
    queries, cache_pool, lengths, block_table, residual, norm_gain, uv_weight, out_weight, gate_weight, up_weight
):
    gain = norm_gain.reshape(D // 128, 128)
    vmem = pl.BlockSpec(memory_space=pltpu.VMEM)
    smem = pl.BlockSpec(memory_space=pltpu.SMEM)
    hbm = pl.BlockSpec(memory_space=pl.ANY)
    dma = pltpu.SemaphoreType.DMA
    mixed, activ = pl.pallas_call(
        kernel,
        out_shape=(pltpu.VMEM((SLOTS, D), BF16), pltpu.VMEM((HID, N * SLOTS), BF16)),
        in_specs=[smem, smem] + [hbm] * 8,
        out_specs=(vmem, vmem),
        scratch_shapes=[
            pltpu.VMEM((SLOTS, HEADS, WIDTH), BF16),
            pltpu.VMEM((SLOTS, PAGE, WIDTH), BF16),
            pltpu.VMEM((SLOTS, D), BF16),
            pltpu.VMEM((2, LAT, 128), BF16),
            pltpu.VMEM((COLS, N * LANES), BF16),
            pltpu.VMEM((HID, D), BF16),
            pltpu.VMEM((HID, D), BF16),
            pltpu.VMEM((D // 128, 128), BF16),
            pltpu.VMEM((D // 128, 128), F32),
            pltpu.VMEM((SLOTS // 4, 4, TOK), F32),
            pltpu.VMEM((LAT // 128, SLOTS * HEADS, 128), F32),
            pltpu.VMEM((NC, N, 2 * SL, LAT), BF16),
            pltpu.VMEM((NC, N, 2 * SL, LAT), BF16),
            pltpu.VMEM((N, SLOTS, LANES), BF16),
            pltpu.VMEM((N, SLOTS, LANES), BF16),
            pltpu.VMEM((NC, N, RC, LANES), BF16),
            pltpu.VMEM((NC, N, COLS, RC), BF16),
            pltpu.VMEM((N, 2 * HID, COLS), BF16),
            pltpu.VMEM((NC, COLS, RC), F32),
            pltpu.VMEM((NC, 2 * HID, RC), F32),
            pltpu.VMEM((NC, 8, RC), F32),
            pltpu.VMEM((NC, N, SLOTS, COLS), F32),
            pltpu.VMEM((NC, SLOTS, RC), BF16),
            pltpu.VMEM((NC * RC, NC * RC), BF16),
            pltpu.VMEM((NC, HID, NC * RC), F32),
            dma((9,)),
            dma((NC + 1,)),
            dma,
            dma,
            dma((NC,)),
            dma((NC,)),
            dma((2, NC)),
            dma((2, NC, 4)),
            dma((2, NC, 16)),
            dma((2, NC, 16)),
        ],
        compiler_params=pltpu.CompilerParams(
            collective_id=0, has_side_effects=True, vmem_limit_bytes=60 * 1024 * 1024
        ),
        cost_estimate=pl.CostEstimate(flops=7 * 10**9, bytes_accessed=15 * 10**6, transcendentals=10**6),
    )(
        lengths, block_table.T, queries, cache_pool, residual, gain, uv_weight,
        out_weight.T, gate_weight.T, up_weight.T,
    )
    mixed, activ = pl.pallas_call(
        hand_out,
        out_shape=(
            jax.ShapeDtypeStruct((SLOTS, D), BF16),
            jax.ShapeDtypeStruct((HID, N * SLOTS), BF16),
        ),
        in_specs=[vmem, vmem],
        out_specs=(hbm, hbm),
        scratch_shapes=[dma((2,))],
    )(pltpu.with_memory_space_constraint(mixed, pltpu.VMEM), pltpu.with_memory_space_constraint(activ, pltpu.VMEM))
    return mixed, activ.T


def solution(mesh):
    placed = (
        P(("group", "rank"), None, None),
        P(("group", "rank"), None, None),
        P(("group", "rank")),
        P(("group", "rank"), None),
        P(("group", "rank"), None),
        P(),
        P("rank", None, None),
        P(None, "rank"),
        P(None, "rank"),
        P(None, "rank"),
    )
    return jax.shard_map(
        per_device,
        mesh=mesh,
        in_specs=placed,
        out_specs=(P(("group", "rank"), None), P("group", "rank")),
        check_vma=False,
    )
```
